32 devices in a mesh: tm: 4 (over x, core), space: 8 (over z, y).
Axes of the slice: x: 2, y: 2, z: 4, core: 2. Of those that a mesh axis runs over, the one named last changes fastest.
Arguments:
- adjoint_field: float32 [512, 24, 9216], P('tm', 'space'), may hold values from -6 to 6
- absorption: float32 [24, 9216], P('space'), may hold values from 0.25 to 2
- mode_rates: float32 [16], replicated, may hold values from 0.1 to 40
- mode_weights: float32 [16], replicated, may hold values from 0.1 to 0.5
Outputs:
- adjoint_image: float32 [512, 24, 9216], P('tm', 'space')
The draws below stay inside these ranges and needn't reach their ends.
All inputs are finite; a program needn't handle non-finite values.
Results may differ from the reference program's by a relative error of at most 0.0001.
Values sent between devices are 32-bit elements; how exact they have to be, the bound alone decides.
No kernel may reach another device: no remote copies, remote signals or barrier semaphores. Data moves between devices by JAX's collectives and lax.ppermute only.
A program may use at most 192 MiB of HBM per device.

```python
import math
import jax
import jax.numpy as jnp
from jax import lax

NY = 96
BAND = 16
MODES = 16
NZ = 24
TIME = 512
PLANE = 9216


def levels(key, shape, pieces, low, high):
    loudness = 1.0
    for axis_at, shards_of in pieces:
        steps = jax.random.uniform(jax.random.fold_in(jax.random.fold_in(key, 6), axis_at), (shards_of,), jnp.float32, low / len(pieces), high / len(pieces))
        loudness = loudness * jnp.repeat(jnp.exp(steps), shape[axis_at] // shards_of).reshape((-1,) + (1,) * (len(shape) - 1 - axis_at))
    return loudness


def normal_values(rng, shape, deviation, limit, cuts=(), kind=jnp.bfloat16):
    gain = levels(rng, shape, cuts, -0.22, 0.18) if cuts else 1.0
    entries = jax.random.normal(rng, shape, jnp.float32) * deviation * gain
    return jnp.minimum(jnp.maximum(entries, -limit), limit).astype(kind)


def setup_inputs(seed: int = 0) -> dict:
    arg_keys = jax.random.split(jax.random.key(seed), 5)
    adjoint_field = normal_values(arg_keys[0], (TIME, NZ, PLANE), 1.0, 6.0, ((0, 4), (1, 8)), jnp.float32)
    absorption = jnp.clip(0.25 + 1.75 * jax.random.uniform(arg_keys[1], (NZ, PLANE), jnp.float32) ** levels(arg_keys[1], (NZ, PLANE), ((0, 8),), -0.2, 0.2), 0.25, 2.0)
    mode_rates = jnp.clip(jnp.exp(jax.random.uniform(arg_keys[2], (MODES,), jnp.float32, math.log(0.1), math.log(40.0))), 0.1, 40.0)
    mode_weights = jnp.clip(jnp.exp(jax.random.uniform(arg_keys[3], (MODES,), jnp.float32, math.log(0.1), math.log(0.5))), 0.1, 0.5)
    return {"adjoint_field": adjoint_field, "absorption": absorption, "mode_rates": mode_rates, "mode_weights": mode_weights}


DIFFUSION = 0.2
ORDER_EXP = 0.4
STENCIL = (-1.0 / 12.0, 16.0 / 12.0, -30.0 / 12.0, 16.0 / 12.0, -1.0 / 12.0)

def caputo_weights(count):
    steps_idx = jnp.arange(count, dtype=jnp.float32)
    increments = (steps_idx + 1.0) ** ORDER_EXP - steps_idx ** ORDER_EXP
    earlier = jnp.concatenate([jnp.zeros((1,), jnp.float32), increments[:-1]])
    return increments - earlier

def mode_tables(mode_rates, mode_weights, total_steps):
    scaled = mode_rates / total_steps
    decays = jnp.exp(-scaled)
    mode_gain = mode_weights * jnp.sqrt(-jnp.expm1(-2.0 * scaled))
    return (scaled, decays, mode_gain)

def band_weights(scaled, mode_gain):
    offsets = jnp.arange(BAND, dtype=jnp.float32)
    far_part = lax.optimization_barrier(jnp.sum(mode_gain[:, None] * jnp.exp(-scaled[:, None] * offsets[None, :]), axis=0))
    return caputo_weights(BAND) - far_part

def plane_masks(row_len, plane_len):
    column = jnp.arange(plane_len, dtype=jnp.int32) % row_len
    return [((column + offset >= 0) & (column + offset < row_len)).astype(jnp.float32) for offset in (-2, -1, 1, 2)]

def laplacian(padded, slab_depth, row_len):
    plane_len = padded.shape[-1]
    center = padded[..., 2:2 + slab_depth, :]
    summed = 3.0 * STENCIL[2] * center
    for offset in (-2, -1, 1, 2):
        summed = summed + STENCIL[offset + 2] * padded[..., 2 + offset:2 + offset + slab_depth, :]
    widths = [(0, 0)] * (center.ndim - 1) + [(2 * row_len, 2 * row_len)]
    spread = jnp.pad(center, widths)
    y_masks = plane_masks(row_len, plane_len)
    for position, offset in enumerate((-2, -1, 1, 2)):
        weight = STENCIL[offset + 2]
        anchor = 2 * row_len + offset * row_len
        summed = summed + weight * spread[..., anchor:anchor + plane_len]
        anchor = 2 * row_len + offset
        summed = summed + weight * y_masks[position] * spread[..., anchor:anchor + plane_len]
    return summed

def reference(adjoint_field, absorption, mode_rates, mode_weights):
    scaled, decays, mode_gain = mode_tables(mode_rates, mode_weights, TIME)
    weights = band_weights(scaled, mode_gain)

    def advance(state_pair, current):
        mode_sums, window = state_pair
        mode_sums = current[None] + decays[:, None, None] * mode_sums
        stacked = jnp.concatenate([current[None], window], axis=0)
        history = jnp.tensordot(weights, stacked, axes=1, precision=lax.Precision.HIGHEST)
        history = history + jnp.tensordot(mode_gain, mode_sums, axes=1, precision=lax.Precision.HIGHEST)
        padded = jnp.pad(current, ((2, 2), (0, 0)))
        outcome = history + absorption * current - DIFFUSION * laplacian(padded, NZ, NY)
        return ((mode_sums, stacked[:-1]), outcome)
    initial = (jnp.zeros((MODES, NZ, PLANE), jnp.float32), jnp.zeros((BAND - 1, NZ, PLANE), jnp.float32))
    final_state, images = lax.scan(advance, initial, adjoint_field, reverse=True)
    return images
```

```python
import functools

import jax
import jax.numpy as jnp
from jax import lax
from jax.experimental import pallas as pl
from jax.experimental.pallas import tpu as pltpu
from jax.sharding import PartitionSpec as P

NY = 96
BAND = 16

DIFFUSION = 0.2
ORDER_EXP = 0.4
STENCIL = (-1.0 / 12.0, 16.0 / 12.0, -30.0 / 12.0, 16.0 / 12.0, -1.0 / 12.0)
NEAR = -DIFFUSION * STENCIL[1]
FAR = -DIFFUSION * STENCIL[0]
OFFSETS = (-2, -1, 1, 2)
ROWS = 8
VMEM_LIMIT = 48 * 1024 * 1024


def tied(value, *others):
    return lax.optimization_barrier((value, *others))[0]


def caputo_weights(count):
    steps_idx = jnp.arange(count, dtype=jnp.float32)
    increments = (steps_idx + 1.0) ** ORDER_EXP - steps_idx**ORDER_EXP
    earlier = jnp.concatenate([jnp.zeros((1,), jnp.float32), increments[:-1]])
    return increments - earlier


def mode_tables(mode_rates, mode_weights, total_steps):
    scaled = mode_rates / total_steps
    mode_gain = mode_weights * jnp.sqrt(-jnp.expm1(-2.0 * scaled))
    return scaled, mode_gain


def history_tables(scaled, mode_gain, steps):
    span = steps + BAND
    lag = jnp.arange(span, dtype=jnp.int32)[None, :] - jnp.arange(steps, dtype=jnp.int32)[:, None]
    lag_clip = jnp.maximum(lag, 0).astype(jnp.float32)
    far = jnp.sum(
        mode_gain[:, None, None] * jnp.exp(-scaled[:, None, None] * lag_clip[None]), axis=0
    )
    onehot = (lag[None] == jnp.arange(BAND, dtype=jnp.int32)[:, None, None]).astype(jnp.float32)
    near = jnp.sum(caputo_weights(BAND)[:, None, None] * onehot, axis=0)
    own = near + jnp.where(lag >= BAND, far, 0.0)
    ahead = jnp.where((lag >= 0) & (lag < BAND), near - far, 0.0)
    pos = jnp.arange(steps, dtype=jnp.float32)
    projector = jnp.exp(-scaled[:, None] * pos[None, :])
    remote_gain = mode_gain[None, :] * jnp.exp(-scaled[None, :] * (steps - pos)[:, None])
    return own[:, :steps], ahead[:, steps:], projector, remote_gain


def dot(a, b):
    return jnp.dot(a, b, precision=lax.Precision.HIGHEST, preferred_element_type=jnp.float32)


def tile_of(plane):
    for count in range(4, plane + 1):
        if plane % count == 0 and (plane // count) % 128 == 0:
            return plane // count
    return plane


def sums_kernel(projector, field, sums):
    sums[...] = dot(projector[...], field[...])


def mode_sums(projector, field):
    depth, steps, plane = field.shape
    modes = projector.shape[0]
    tile = tile_of(plane)
    return pl.pallas_call(
        sums_kernel,
        grid=(depth, plane // tile),
        in_specs=[
            pl.BlockSpec((modes, steps), lambda p, c: (0, 0)),
            pl.BlockSpec((None, steps, tile), lambda p, c: (p, 0, c)),
        ],
        out_specs=pl.BlockSpec((None, modes, tile), lambda p, c: (p, 0, c)),
        out_shape=jax.ShapeDtypeStruct((depth, modes, plane), jnp.float32),
        compiler_params=pltpu.CompilerParams(vmem_limit_bytes=VMEM_LIMIT),
        cost_estimate=pl.CostEstimate(
            flops=12 * field.size * modes, bytes_accessed=4 * field.size, transcendentals=0
        ),
        name="mode_sums",
    )(projector, field)


def history_kernel(inner, outer, gain, field, head, later, history):
    history[...] = (
        dot(inner[...], field[...]) + dot(outer[...], head[...]) + dot(gain[...], later[...])
    )


def history_of(inner, outer, gain, field, head, later):
    depth, steps, plane = field.shape
    tile = tile_of(plane)
    whole = lambda p, c: (0, 0)
    part = lambda p, c: (p, 0, c)
    return pl.pallas_call(
        history_kernel,
        grid=(depth, plane // tile),
        in_specs=[
            pl.BlockSpec(inner.shape, whole),
            pl.BlockSpec(outer.shape, whole),
            pl.BlockSpec(gain.shape, whole),
            pl.BlockSpec((None, steps, tile), part),
            pl.BlockSpec((None, head.shape[1], tile), part),
            pl.BlockSpec((None, later.shape[1], tile), part),
        ],
        out_specs=pl.BlockSpec((None, steps, tile), part),
        out_shape=jax.ShapeDtypeStruct(field.shape, jnp.float32),
        compiler_params=pltpu.CompilerParams(vmem_limit_bytes=VMEM_LIMIT),
        cost_estimate=pl.CostEstimate(
            flops=12 * field.size * (steps + 2 * BAND),
            bytes_accessed=8 * field.size,
            transcendentals=0,
        ),
        name="history",
    )(inner, outer, gain, field, head, later)


def local_kernel(depth, shifts, outer_plane, masks, absorption, field, near, out_side, beyond, history, image):
    plane = field.shape[-1]
    first = outer_plane[0] == 0
    for p in range(depth):
        cells = field[p]
        total = history[p] + (absorption[p][None, :] - 3.0 * DIFFUSION * STENCIL[2]) * cells
        for row, shift in enumerate(shifts):
            total = total + masks[row][None, :] * pltpu.roll(cells, (-shift) % plane, 1)
        for offset in OFFSETS:
            if 0 <= p + offset < depth:
                total = total + (-DIFFUSION * STENCIL[offset + 2]) * field[p + offset]
        image[p] = total
    inner_plane = depth - 1 - outer_plane[0]
    image[outer_plane[0]] += NEAR * beyond[...] + FAR * out_side[...]
    middle = jnp.where(first, 1, depth - 2)
    image[middle] += FAR * beyond[...]
    image[inner_plane] += FAR * near[...]


def local_terms(outer_plane, masks, absorption, field, near, out_side, beyond, history, shifts):
    depth, steps, plane = field.shape
    slab = pl.BlockSpec((depth, ROWS, plane), lambda t, s: (0, t, 0))
    single = pl.BlockSpec((ROWS, plane), lambda t, s: (t, 0))
    return pl.pallas_call(
        functools.partial(local_kernel, depth, shifts),
        grid_spec=pltpu.PrefetchScalarGridSpec(
            num_scalar_prefetch=1,
            grid=(steps // ROWS,),
            in_specs=[
                pl.BlockSpec(masks.shape, lambda t, s: (0, 0)),
                pl.BlockSpec(absorption.shape, lambda t, s: (0, 0)),
                slab,
                single,
                single,
                single,
                slab,
            ],
            out_specs=slab,
        ),
        out_shape=jax.ShapeDtypeStruct(field.shape, jnp.float32),
        input_output_aliases={7: 0},
        compiler_params=pltpu.CompilerParams(vmem_limit_bytes=VMEM_LIMIT),
        cost_estimate=pl.CostEstimate(
            flops=40 * field.size, bytes_accessed=16 * field.size, transcendentals=0
        ),
        name="local_terms",
    )(outer_plane, masks, absorption, field, near, out_side, beyond, history)


def inner_kernel(planes, beside, image, out):
    weight = jnp.where(pl.program_id(1) == 0, NEAR, FAR)
    out[...] = image[...] + weight * beside[...]


def add_inner(planes, beside, image, start):
    depth, steps, plane = image.shape
    count = beside.shape[0]
    at = pl.BlockSpec((None, ROWS, plane), lambda t, g, s: (s[g], start // ROWS + t, 0))
    return pl.pallas_call(
        inner_kernel,
        grid_spec=pltpu.PrefetchScalarGridSpec(
            num_scalar_prefetch=1,
            grid=(count // ROWS, 2),
            in_specs=[pl.BlockSpec((ROWS, plane), lambda t, g, s: (t, 0)), at],
            out_specs=at,
        ),
        out_shape=jax.ShapeDtypeStruct(image.shape, jnp.float32),
        input_output_aliases={2: 0},
        compiler_params=pltpu.CompilerParams(vmem_limit_bytes=VMEM_LIMIT),
        cost_estimate=pl.CostEstimate(
            flops=4 * beside.size, bytes_accessed=20 * beside.size, transcendentals=0
        ),
        name="add_inner",
    )(planes, beside, image)


def cuts(steps, pieces):
    marks = [ROWS * round(steps * i / pieces / ROWS) for i in range(pieces + 1)]
    return list(zip(marks[:-1], marks[1:]))


def per_device(adjoint_field, absorption, mode_rates, mode_weights):
    steps, depth, plane = adjoint_field.shape
    groups = lax.axis_size("tm")
    slabs = lax.axis_size("space")
    pairs = slabs // 2
    me = lax.axis_index("space")
    odd = me % 2
    field = adjoint_field.transpose(1, 0, 2)

    swap = [(i, i ^ 1) for i in range(slabs)]
    outward = [(i, i - 2 if i % 2 == 0 else i + 2) for i in range(slabs)]
    outward = [(a, b) for a, b in outward if 0 <= b < slabs]
    onward = [(i, i + 2 if i % 2 == 0 else i - 2) for i in range(slabs)]
    onward = [(a, b) for a, b in onward if 0 <= b < slabs]

    def rank(i):
        return i // 2 if i % 2 == 0 else pairs - 1 - i // 2

    my_rank = jnp.where(odd == 0, me // 2, pairs - 1 - me // 2)
    partner_rank = jnp.where(odd == 1, me // 2, pairs - 1 - me // 2)

    outer_at = jnp.where(odd == 0, 0, depth - 1).astype(jnp.int32)
    inner_at = depth - 1 - outer_at

    def piece(at, lo, hi):
        return lax.dynamic_slice(field, (at, lo, 0), (1, hi - lo, plane))[0]

    halves = cuts(steps, 2)
    quarters = cuts(steps, pairs)
    relay_end = quarters[-1][0]

    mid = [lax.slice(field, (1, lo, 0), (2, hi, plane))[0] for lo, hi in halves]
    y_mid0 = lax.ppermute(mid[0], "space", swap)
    outer_part = piece(outer_at, 0, relay_end)
    outer_part = tied(outer_part, mid[0])
    relayed = lax.ppermute(outer_part, "space", outward)
    mid1 = tied(mid[1], outer_part)
    y_mid1 = lax.ppermute(mid1, "space", swap)
    head = lax.slice(field, (0, 0, 0), (depth, BAND, plane))
    head = tied(head, mid1)
    back = [(i, i - 1) for i in range(1, groups)]
    next_head = lax.ppermute(head, "tm", back)

    rates, weights = lax.optimization_barrier((mode_rates, mode_weights, head))[:2]
    scaled, mode_gain = mode_tables(rates, weights, steps * groups)
    inner, outer, projector, remote_gain = history_tables(scaled, mode_gain, steps)
    sums = mode_sums(projector, field)
    block_decay = jnp.exp(-scaled * steps)[None, :, None]
    later = lax.ppermute(sums, "tm", back)

    y_mid0 = tied(y_mid0, sums)
    z_mid0 = lax.ppermute(y_mid0, "space", onward)

    def outer_send(q, *after):
        lo, hi = quarters[q]
        own = piece(outer_at, lo, hi)
        if q < pairs - 1:
            own = jnp.where(q < pairs - 1 - my_rank, relayed[lo:hi], own)
        own = tied(own, *after)
        route = [(i, i ^ 1) for i in range(slabs) if q != pairs - 1 - rank(i)]
        return lax.ppermute(own, "space", route)

    def outer_onward(q, got):
        route = [
            (a, b) for a, b in onward if q > pairs - 1 - rank(a ^ 1)
        ]
        return lax.ppermute(got, "space", route) if route else jnp.zeros_like(got)

    y_out = [outer_send(0, y_mid0)]
    for _ in range(groups - 2):
        later = lax.ppermute(sums + block_decay * later, "tm", back)
    z_mid1 = lax.ppermute(y_mid1, "space", onward)
    y_out.append(outer_send(1, y_mid1))
    history = history_of(inner, outer, remote_gain, field, next_head, later)
    z_out = []
    for q in range(2, pairs):
        y_out.append(outer_send(q, y_out[q - 2]))
    for q in range(pairs):
        z_out.append(outer_onward(q, y_out[q]))
    inner_cuts = [(0, steps // 2), (steps // 2, steps - 2 * ROWS), (steps - 2 * ROWS, steps)]
    y_in = []
    waits = [y_out[pairs - 2], y_out[pairs - 1]]
    for (lo, hi) in inner_cuts:
        src = tied(piece(inner_at, lo, hi), waits[len(y_in)])
        y_in.append(lax.ppermute(src, "space", swap))
        waits.append(y_in[-1])

    near = jnp.concatenate([y_mid0, y_mid1], axis=0)
    out_side = jnp.concatenate([z_mid0, z_mid1], axis=0)
    beyond = jnp.concatenate(
        [jnp.where(q < pairs - 1 - partner_rank, y_out[q], z_out[q]) for q in range(pairs)], axis=0
    )
    column = jnp.arange(plane, dtype=jnp.int32)
    row_pos = column % NY
    masks = [
        jnp.where((row_pos + o >= 0) & (row_pos + o < NY), -DIFFUSION * STENCIL[o + 2], 0.0) for o in OFFSETS
    ] + [
        jnp.where((column + o * NY >= 0) & (column + o * NY < plane), -DIFFUSION * STENCIL[o + 2], 0.0)
        for o in OFFSETS
    ]
    masks = jnp.stack(masks).astype(jnp.float32)
    shifts = tuple(OFFSETS) + tuple(o * NY for o in OFFSETS)
    image = local_terms(
        outer_at[None], masks, absorption, field, near, out_side, beyond, history, shifts
    )
    planes = jnp.stack([inner_at, jnp.where(odd == 0, depth - 2, 1).astype(jnp.int32)])
    for (lo, hi), beside in zip(inner_cuts, y_in):
        image = add_inner(planes, beside, image, lo)
    return image.transpose(1, 0, 2)


def solution(mesh):
    return jax.shard_map(
        per_device,
        mesh=mesh,
        in_specs=(P("tm", "space", None), P("space", None), P(), P()),
        out_specs=P("tm", "space", None),
        check_vma=False,
    )
```

```python
import functools
import math

import jax
import jax.numpy as jnp
from jax import lax
from jax.experimental import pallas as pl
from jax.experimental.pallas import tpu as pltpu
from jax.sharding import PartitionSpec as P
import numpy as np

NY = 96
BAND = 16

DIFFUSION = 0.2
ORDER_EXP = 0.4
STENCIL = (-1.0 / 12.0, 16.0 / 12.0, -30.0 / 12.0, 16.0 / 12.0, -1.0 / 12.0)
NEAR = -DIFFUSION * STENCIL[1]
FAR = -DIFFUSION * STENCIL[0]
OFFSETS = (-2, -1, 1, 2)
ROWS = 8
VMEM_LIMIT = 48 * 1024 * 1024
SHORT = pl.CostEstimate(flops=1, bytes_accessed=1, transcendentals=0)

OUTER, INNER, MIDDLE, RANK, PARTNER_RANK = range(5)


def mode_tables(mode_rates, mode_weights, total_steps):
    scaled = mode_rates / total_steps
    mode_gain = mode_weights * jnp.sqrt(-jnp.expm1(-2.0 * scaled))
    return scaled, mode_gain


def caputo_weights():
    grown = np.arange(BAND + 1, dtype=np.float64) ** ORDER_EXP
    increments = grown[1:] - grown[:-1]
    return [float(w) for w in np.diff(increments, prepend=0.0)]


def dot(a, b):
    return jnp.dot(a, b, precision=lax.Precision.HIGHEST, preferred_element_type=jnp.float32)


def tile_of(plane):
    for count in range(4, plane + 1):
        if plane % count == 0 and (plane // count) % 128 == 0:
            return plane // count
    return plane


def sums_kernel(scaled, field, sums, projector):
    modes, steps = projector.shape

    @pl.when((pl.program_id(0) == 0) & (pl.program_id(1) == 0))
    def _():
        pos = lax.broadcasted_iota(jnp.int32, (1, steps), 1).astype(jnp.float32)
        for j in range(modes):
            projector[j : j + 1, :] = jnp.exp(-scaled[j] * pos)

    sums[...] = dot(projector[...], field[...])


def mode_sums(scaled, field):
    depth, steps, plane = field.shape
    modes = scaled.shape[0]
    tile = tile_of(plane)
    return pl.pallas_call(
        sums_kernel,
        grid=(depth, plane // tile),
        in_specs=[
            pl.BlockSpec(memory_space=pltpu.SMEM),
            pl.BlockSpec((None, steps, tile), lambda p, c: (p, 0, c)),
        ],
        out_specs=pl.BlockSpec((None, modes, tile), lambda p, c: (p, 0, c)),
        out_shape=jax.ShapeDtypeStruct((depth, modes, plane), jnp.float32),
        scratch_shapes=[pltpu.VMEM((modes, steps), jnp.float32)],
        compiler_params=pltpu.CompilerParams(vmem_limit_bytes=VMEM_LIMIT),
        cost_estimate=SHORT,
        name="mode_sums",
    )(scaled, field)


def carry_kernel(steps, scaled, sums, later, total):
    for j in range(total.shape[0]):
        decay = jnp.exp(jnp.full((1, total.shape[1]), -scaled[j] * steps, jnp.float32))
        total[j : j + 1, :] = sums[j : j + 1, :] + decay * later[j : j + 1, :]


def carried(scaled, steps, sums, later):
    depth, _, plane = sums.shape
    modes = scaled.shape[0]
    part = pl.BlockSpec((None, modes, plane), lambda p: (p, 0, 0))
    return pl.pallas_call(
        functools.partial(carry_kernel, steps),
        grid=(depth,),
        in_specs=[pl.BlockSpec(memory_space=pltpu.SMEM), part, part],
        out_specs=part,
        out_shape=jax.ShapeDtypeStruct((depth, modes, plane), jnp.float32),
        cost_estimate=SHORT,
        name="carried",
    )(scaled, sums, later)


def fill_tables(steps, aways, scaled, mode_gain, scaled_row, gain_row, table):
    near_weights = caputo_weights()
    modes = scaled.shape[0]

    def lags(columns, ahead):
        row = lax.broadcasted_iota(jnp.int32, (steps, columns), 0)
        return lax.broadcasted_iota(jnp.int32, (steps, columns), 1) - row + ahead

    def far_of(lag):
        distance = jnp.maximum(lag, 0).astype(jnp.float32)
        far = jnp.zeros(lag.shape, jnp.float32)
        for j in range(modes):
            far = far + mode_gain[j] * jnp.exp(-scaled[j] * distance)
        return far

    def near_of(lag):
        near = jnp.zeros(lag.shape, jnp.float32)
        for k, weight in enumerate(near_weights):
            near = jnp.where(lag == k, weight, near)
        return near

    lag = lags(steps, 0)
    table[:, :steps] = jnp.where(lag >= BAND, far_of(lag), near_of(lag))
    lag = lags(BAND, steps)
    table[:, steps : steps + BAND] = jnp.where(lag < BAND, near_of(lag) - far_of(lag), 0.0)
    row = lax.broadcasted_iota(jnp.int32, (steps, modes), 0)
    for k, away in enumerate(aways):
        at = steps + BAND + k * modes
        distance = (away * steps - row).astype(jnp.float32)
        table[:, at : at + modes] = gain_row[...] * jnp.exp(-scaled_row[...] * distance)


def history_kernel(aways, scaled, mode_gain, scaled_row, gain_row, field, *refs):
    parts, (before, image, table, stacked) = refs[: 1 + len(aways)], refs[1 + len(aways) :]
    steps = field.shape[0]

    @pl.when((pl.program_id(0) == 0) & (pl.program_id(1) == 0))
    def _():
        fill_tables(steps, aways, scaled, mode_gain, scaled_row, gain_row, table)

    stacked[:steps, :] = field[...]
    at = steps
    for part in parts:
        stacked[at : at + part.shape[0], :] = part[...]
        at += part.shape[0]
    image[...] = before[...] + dot(table[...], stacked[...])


def add_history(scaled, mode_gain, field, head, aways, later, image):
    depth, steps, plane = field.shape
    modes = scaled.shape[0]
    tile = tile_of(plane)
    operands = (field, head, *later)
    rows = sum(array.shape[1] for array in operands)
    smem = pl.BlockSpec(memory_space=pltpu.SMEM)
    whole = pl.BlockSpec((1, modes), lambda p, c: (0, 0))
    part = lambda p, c: (p, 0, c)
    return pl.pallas_call(
        functools.partial(history_kernel, aways),
        grid=(depth, plane // tile),
        in_specs=[
            smem,
            smem,
            whole,
            whole,
            *[pl.BlockSpec((None, array.shape[1], tile), part) for array in (*operands, image)],
        ],
        out_specs=pl.BlockSpec((None, steps, tile), part),
        out_shape=jax.ShapeDtypeStruct(field.shape, jnp.float32),
        input_output_aliases={4 + len(operands): 0},
        scratch_shapes=[pltpu.VMEM((steps, rows), jnp.float32), pltpu.VMEM((rows, tile), jnp.float32)],
        compiler_params=pltpu.CompilerParams(vmem_limit_bytes=VMEM_LIMIT),
        cost_estimate=SHORT,
        name="add_history",
    )(scaled, mode_gain, scaled[None], mode_gain[None], *operands, image)


def copy_rows(source, out, sems):
    pieces = [pl.ds(k * ROWS, ROWS) for k in range(out.shape[0] // ROWS)]
    copies = [
        pltpu.make_async_copy(source.at[rows], out.at[rows], sems.at[k]) for k, rows in enumerate(pieces)
    ]
    for copy in copies:
        copy.start()
    for copy in copies:
        copy.wait()


def staged(kernel, name, shape, device, *arrays):
    return pl.pallas_call(
        kernel,
        in_specs=[pl.BlockSpec(memory_space=pltpu.SMEM)]
        + [pl.BlockSpec(memory_space=pl.ANY)] * len(arrays),
        out_specs=pl.BlockSpec(memory_space=pltpu.VMEM),
        out_shape=pltpu.VMEM(shape, jnp.float32),
        scratch_shapes=[pltpu.SemaphoreType.DMA((math.prod(shape[:-1]) // ROWS,))],
        cost_estimate=SHORT,
        name=name,
    )(device, *arrays)


def rows_kernel(which, lo, device, field, out, sems):
    copy_rows(field.at[device[which], pl.ds(lo, out.shape[0])], out, sems)


def middle_kernel(lo, field, token, out, sems):
    copy_rows(field.at[1, pl.ds(lo, out.shape[0])], out, sems)


def middle_rows(field, token, lo, hi):
    shape = (hi - lo, field.shape[-1])
    return pl.pallas_call(
        functools.partial(middle_kernel, lo),
        in_specs=[pl.BlockSpec(memory_space=pl.ANY)] * 2,
        out_specs=pl.BlockSpec(memory_space=pltpu.VMEM),
        out_shape=pltpu.VMEM(shape, jnp.float32),
        scratch_shapes=[pltpu.SemaphoreType.DMA((shape[0] // ROWS,))],
        cost_estimate=SHORT,
        name="middle_rows",
    )(field, token)


def rows_of(device, which, field, lo, hi):
    kernel = functools.partial(rows_kernel, which, lo)
    return staged(kernel, "rows_of", (hi - lo, field.shape[-1]), device, field)


def pick_kernel(last, relayed_lo, own_lo, device, field, relayed, out, sems):
    count = out.shape[0]

    @pl.when(device[RANK] < last)
    def _():
        copy_rows(relayed.at[pl.ds(relayed_lo, count)], out, sems)

    @pl.when(device[RANK] >= last)
    def _():
        copy_rows(field.at[device[OUTER], pl.ds(own_lo, count)], out, sems)


def picked_rows(device, field, relayed, last, relayed_lo, own_lo, count):
    kernel = functools.partial(pick_kernel, last, relayed_lo, own_lo)
    return staged(kernel, "picked_rows", (count, field.shape[-1]), device, field, relayed)


def head_kernel(device, field, out, sems):
    per_plane = BAND // ROWS
    for p in range(out.shape[0]):
        copy_rows(field.at[p, pl.ds(0, BAND)], out.at[p], sems.at[pl.ds(p * per_plane, per_plane)])


def head_of(device, field):
    depth, _, plane = field.shape
    return staged(head_kernel, "head_of", (depth, BAND, plane), device, field)


def join_kernel(device, *refs):
    arrays, (out, sems) = refs[:-2], refs[-2:]
    at = 0
    for array in arrays:
        rows = array.shape[0]
        copy_rows(array, out.at[pl.ds(at, rows)], sems.at[pl.ds(at // ROWS, rows // ROWS)])
        at += rows


def joined(device, arrays):
    shape = (sum(array.shape[0] for array in arrays), arrays[0].shape[1])
    return staged(join_kernel, "joined", shape, device, *arrays)


def block_rows(*edges):
    return 2 * ROWS if all(edge % (2 * ROWS) == 0 for edge in edges) else ROWS


def plane_kernel(depth, shifts, absorption, field, *refs):
    image, masks = refs[-2:]
    plane = field.shape[-1]

    @pl.when(pl.program_id(0) == 0)
    def _():
        column = lax.broadcasted_iota(jnp.int32, (1, plane), 1)
        row_pos = column % NY
        for at, offset in enumerate(OFFSETS):
            weight = -DIFFUSION * STENCIL[offset + 2]
            moved = row_pos + offset
            masks[at : at + 1, :] = jnp.where((moved >= 0) & (moved < NY), weight, 0.0)
            at += len(OFFSETS)
            moved = column + offset * NY
            masks[at : at + 1, :] = jnp.where((moved >= 0) & (moved < plane), weight, 0.0)

    for p in range(depth):
        cells = field[p]
        total = (absorption[p][None, :] - 3.0 * DIFFUSION * STENCIL[2]) * cells
        for row, shift in enumerate(shifts):
            total = total + masks[row][None, :] * pltpu.roll(cells, (-shift) % plane, 1)
        for offset in OFFSETS:
            if 0 <= p + offset < depth:
                total = total + (-DIFFUSION * STENCIL[offset + 2]) * field[p + offset]
        image[p] = total


def plane_terms(token, absorption, field, image, start, end):
    depth, _, plane = field.shape
    shifts = tuple(OFFSETS) + tuple(offset * NY for offset in OFFSETS)
    first = start // ROWS
    slab = pl.BlockSpec((depth, ROWS, plane), lambda t: (0, first + t, 0))
    in_any = pl.BlockSpec(memory_space=pl.ANY)
    started = [] if image is None else [image]
    return pl.pallas_call(
        functools.partial(plane_kernel, depth, shifts),
        grid=((end - start) // ROWS,),
        in_specs=[pl.BlockSpec(absorption.shape, lambda t: (0, 0)), slab, in_any] + [in_any] * len(started),
        out_specs=slab,
        scratch_shapes=[pltpu.VMEM((len(shifts), plane), jnp.float32)],
        out_shape=jax.ShapeDtypeStruct(field.shape, jnp.float32),
        input_output_aliases={3: 0} if started else {},
        compiler_params=pltpu.CompilerParams(vmem_limit_bytes=VMEM_LIMIT),
        cost_estimate=SHORT,
        name="plane_terms",
    )(absorption, field, token, *started)


def halo_kernel(last, device, near, out_side, over_y, over_z, before, image):
    beyond = jnp.where(device[PARTNER_RANK] < last, over_y[...], over_z[...])
    outer, middle, inner = device[OUTER], device[MIDDLE], device[INNER]
    image[outer] = before[outer] + NEAR * beyond + FAR * out_side[...]
    image[middle] = before[middle] + FAR * beyond
    image[inner] = before[inner] + FAR * near[...]


def add_halo(device, near, out_side, over_y, over_z, image, last, start, end):
    depth, _, plane = image.shape
    beside = (near, out_side, over_y, over_z)
    rows = block_rows(start, end, *[row for _, row in beside])
    slab = pl.BlockSpec((depth, rows, plane), lambda t, s: (0, start // rows + t, 0))

    def single(row):
        return pl.BlockSpec((rows, plane), lambda t, s: (row // rows + t, 0))

    return pl.pallas_call(
        functools.partial(halo_kernel, last),
        grid_spec=pltpu.PrefetchScalarGridSpec(
            num_scalar_prefetch=1,
            grid=((end - start) // rows,),
            in_specs=[*[single(row) for _, row in beside], slab],
            out_specs=slab,
        ),
        out_shape=jax.ShapeDtypeStruct(image.shape, jnp.float32),
        input_output_aliases={5: 0},
        compiler_params=pltpu.CompilerParams(vmem_limit_bytes=VMEM_LIMIT),
        cost_estimate=SHORT,
        name="add_halo",
    )(device, *[array for array, _ in beside], image)


def inner_kernel(device, beside, image, token, out):
    weight = jnp.where(pl.program_id(1) == 0, NEAR, FAR)
    out[...] = image[...] + weight * beside[...]


def add_inner(device, beside, image, token, start):
    plane = image.shape[-1]
    count = beside.shape[0]
    rows = block_rows(start, count)

    def place(t, g, s):
        return jnp.where(g == 0, s[INNER], s[MIDDLE]), start // rows + t, 0

    at = pl.BlockSpec((None, rows, plane), place)
    return pl.pallas_call(
        inner_kernel,
        grid_spec=pltpu.PrefetchScalarGridSpec(
            num_scalar_prefetch=1,
            grid=(count // rows, 2),
            in_specs=[
                pl.BlockSpec((rows, plane), lambda t, g, s: (t, 0)),
                at,
                pl.BlockSpec(memory_space=pl.ANY),
            ],
            out_specs=at,
        ),
        out_shape=jax.ShapeDtypeStruct(image.shape, jnp.float32),
        input_output_aliases={2: 0},
        compiler_params=pltpu.CompilerParams(vmem_limit_bytes=VMEM_LIMIT),
        cost_estimate=SHORT,
        name="add_inner",
    )(device, beside, image, token)


def cuts(steps, pieces):
    marks = [ROWS * round(steps * i / pieces / ROWS) for i in range(pieces + 1)]
    return list(zip(marks[:-1], marks[1:]))


class Order:
    def __init__(self, token):
        self.token = token

    def __call__(self, value):
        value, self.token = lax.optimization_barrier((value, self.token))
        return value


def per_device(adjoint_field, absorption, mode_rates, mode_weights):
    steps, depth, plane = adjoint_field.shape
    groups = lax.axis_size("tm")
    slabs = lax.axis_size("space")
    pairs = slabs // 2
    me = lax.axis_index("space")
    odd = me % 2
    field = adjoint_field.transpose(1, 0, 2)
    order = Order(mode_rates)

    swap = [(i, i ^ 1) for i in range(slabs)]
    outward = [(i, i - 2 if i % 2 == 0 else i + 2) for i in range(slabs)]
    outward = [(a, b) for a, b in outward if 0 <= b < slabs]
    onward = [(i, i + 2 if i % 2 == 0 else i - 2) for i in range(slabs)]
    onward = [(a, b) for a, b in onward if 0 <= b < slabs]

    def back(distance):
        return [(i, i - distance) for i in range(distance, groups)]


    def rank(i):
        return i // 2 if i % 2 == 0 else pairs - 1 - i // 2

    device = jnp.stack(
        [
            jnp.where(odd == 0, 0, depth - 1),
            jnp.where(odd == 0, depth - 1, 0),
            jnp.where(odd == 0, depth - 2, 1),
            jnp.where(odd == 0, me // 2, pairs - 1 - me // 2),
            jnp.where(odd == 1, me // 2, pairs - 1 - me // 2),
        ]
    ).astype(jnp.int32)

    def send(value, axis, route):
        return lax.ppermute(order(value), axis, route)

    def whole_rows(share):
        return ROWS * round(steps * share / ROWS)

    def between(*marks):
        return list(zip(marks[:-1], marks[1:]))

    mid_cuts = between(0, whole_rows(1 / 2), steps)
    out_cuts = cuts(steps, pairs)
    in_cuts = between(0, whole_rows(5 / 8), whole_rows(7 / 8), steps - ROWS, steps)
    plane_cuts = cuts(steps, 4)
    slots = pairs - 1

    def middle_send(k):
        return send(middle_rows(field, order.token, *mid_cuts[k]), "space", swap)

    def outer_send(j):
        last = slots - j
        lo, hi = out_cuts[j]
        own_lo, own_hi = out_cuts[j + 1]
        first = out_cuts[(slots + 1) // 2][0]
        got, at = (relayed[0], lo) if lo < first else (relayed[1], lo - first)
        return send(
            picked_rows(order(device), field, got, last, at, own_lo, own_hi - own_lo), "space", swap
        )

    def outer_onward(parts):
        route = [(a, b) for a, b in onward if parts[-1] >= slots - rank(a ^ 1)]
        return send(y_out[parts[0]] if len(parts) == 1 else together, "space", route)

    def inner_send(k):
        return send(rows_of(order(device), INNER, field, *in_cuts[k]), "space", swap)

    def relay(lo, hi):
        return send(rows_of(order(device), OUTER, field, lo, hi), "space", outward)

    y_steps = [functools.partial(middle_send, k) for k in range(len(mid_cuts))]
    y_steps += [functools.partial(outer_send, j) for j in range(slots)]
    y_steps += [functools.partial(inner_send, k) for k in range(len(in_cuts))]
    sent = []

    def next_y():
        if len(sent) < len(y_steps):
            sent.append(y_steps[len(sent)]())

    scaled, mode_gain = mode_tables(mode_rates, mode_weights, steps * groups)
    next_y()
    next_y()
    first = out_cuts[(slots + 1) // 2][0]
    relayed = [relay(0, first)]
    head = send(head_of(order(device), field), "tm", back(1))
    sums = mode_sums(order(scaled), field)
    aways = [1]
    later = [send(sums, "tm", back(1))]

    def plane(k, image):
        return order(plane_terms(order.token, absorption, field, image, *plane_cuts[k]))

    image = plane(0, None)
    y_mid = [order(sent[0])]
    z_mid = [send(y_mid[0], "space", onward)]
    relayed[0] = order(relayed[0])
    next_y()
    head = order(head)
    later[0] = order(later[0])
    if first < out_cuts[slots][0]:
        relayed.append(relay(first, out_cuts[slots][0]))
    while 2 * aways[-1] < groups:
        if len(aways) > 1:
            later[-1] = order(later[-1])
        sums = carried(order(scaled), aways[-1] * steps, sums, later[-1])
        aways.append(2 * aways[-1])
        later.append(send(sums, "tm", back(aways[-1])))

    image = plane(1, image)
    y_mid.append(order(sent[1]))
    next_y()
    image = plane(2, image)

    def halo(q, image):
        lo, hi = out_cuts[q]
        over_z = y_out[0] if q == 0 else z_last if q == slots else z_most
        at_z = out_cuts[q - 1][0] if 0 < q < slots else 0
        over_y = (y_out[q], 0) if q < slots else (over_z, 0)
        if q == 0:
            over_z = jnp.zeros_like(over_z)
        for k, (start, end) in enumerate(mid_cuts):
            a, b = max(lo, start), min(hi, end)
            if a < b:
                image = add_halo(
                    order(device), (y_mid[k], a - start), (z_mid[k], a - start), (over_y[0], a - lo),
                    (over_z, at_z + a - lo), image, slots - q, a, b,
                )
        return order(image)

    y_out = []
    def inner(k, image):
        return order(add_inner(device, y_in[k], image, order.token, in_cuts[k][0]))

    for j in range(slots):
        y_out.append(order(sent[2 + j]))
        if j == 0:
            relayed[1:] = order(relayed[1:])
        if j < slots - 1:
            next_y()
        if j == 0:
            z_mid.append(send(y_mid[1], "space", onward))
            image = plane(3, image)
        if j == min(1, slots - 1):
            later[1:] = order(later[1:])
        if j == slots - 2:
            together = joined(order(device), y_out)
    z_mid[0] = order(z_mid[0])
    most = list(range(slots - 1))
    z_most = outer_onward(most) if most else None
    next_y()
    z_mid[1] = order(z_mid[1])
    z_last = outer_onward([slots - 1])
    image = halo(0, image)
    image = order(add_history(order(scaled), mode_gain, field, head, aways, later, image))
    y_in = []
    if most:
        z_most = order(z_most)
    for q in range(1, slots):
        image = halo(q, image)
    y_in.append(order(sent[2 + slots]))
    next_y()
    image = inner(0, image)
    z_last = order(z_last)
    image = halo(slots, image)
    for k in range(1, len(in_cuts)):
        y_in.append(order(sent[2 + slots + k]))
        next_y()
        image = inner(k, image)
    return image.transpose(1, 0, 2)


def solution(mesh):
    return jax.shard_map(
        per_device,
        mesh=mesh,
        in_specs=(P("tm", "space", None), P("space", None), P(), P()),
        out_specs=P("tm", "space", None),
        check_vma=False,
    )
```

```python
import functools
import math

import jax
import jax.numpy as jnp
from jax import lax
from jax.experimental import pallas as pl
from jax.experimental.pallas import tpu as pltpu
from jax.sharding import PartitionSpec as P
import numpy as np

NY = 96
BAND = 16

DIFFUSION = 0.2
ORDER_EXP = 0.4
STENCIL = (-1.0 / 12.0, 16.0 / 12.0, -30.0 / 12.0, 16.0 / 12.0, -1.0 / 12.0)
NEAR = -DIFFUSION * STENCIL[1]
FAR = -DIFFUSION * STENCIL[0]
OFFSETS = (-2, -1, 1, 2)
ROWS = 8
VMEM_LIMIT = 48 * 1024 * 1024
SHORT = pl.CostEstimate(flops=1, bytes_accessed=1, transcendentals=0)

OUTER, INNER, MIDDLE, RANK, PARTNER_RANK = range(5)


def mode_tables(mode_rates, mode_weights, total_steps):
    scaled = mode_rates / total_steps
    mode_gain = mode_weights * jnp.sqrt(-jnp.expm1(-2.0 * scaled))
    return scaled, mode_gain


def caputo_weights():
    grown = np.arange(BAND + 1, dtype=np.float64) ** ORDER_EXP
    increments = grown[1:] - grown[:-1]
    return [float(w) for w in np.diff(increments, prepend=0.0)]


def dot(a, b):
    return jnp.dot(a, b, precision=lax.Precision.HIGHEST, preferred_element_type=jnp.float32)


def tile_of(plane):
    for count in range(4, plane + 1):
        if plane % count == 0 and (plane // count) % 128 == 0:
            return plane // count
    return plane


def sums_kernel(scaled, field, sums, projector):
    modes, steps = projector.shape

    @pl.when((pl.program_id(0) == 0) & (pl.program_id(1) == 0))
    def _():
        pos = lax.broadcasted_iota(jnp.int32, (1, steps), 1).astype(jnp.float32)
        for j in range(modes):
            projector[j : j + 1, :] = jnp.exp(-scaled[j] * pos)

    sums[...] = dot(projector[...], field[...])


def mode_sums(scaled, field):
    depth, steps, plane = field.shape
    modes = scaled.shape[0]
    tile = tile_of(plane)
    return pl.pallas_call(
        sums_kernel,
        grid=(depth, plane // tile),
        in_specs=[
            pl.BlockSpec(memory_space=pltpu.SMEM),
            pl.BlockSpec((None, steps, tile), lambda p, c: (p, 0, c)),
        ],
        out_specs=pl.BlockSpec((None, modes, tile), lambda p, c: (p, 0, c)),
        out_shape=jax.ShapeDtypeStruct((depth, modes, plane), jnp.float32),
        scratch_shapes=[pltpu.VMEM((modes, steps), jnp.float32)],
        compiler_params=pltpu.CompilerParams(vmem_limit_bytes=VMEM_LIMIT),
        cost_estimate=SHORT,
        name="mode_sums",
    )(scaled, field)


def carry_kernel(steps, scaled, sums, later, total):
    for j in range(total.shape[0]):
        decay = jnp.exp(jnp.full((1, total.shape[1]), -scaled[j] * steps, jnp.float32))
        total[j : j + 1, :] = sums[j : j + 1, :] + decay * later[j : j + 1, :]


def carried(scaled, steps, sums, later):
    depth, _, plane = sums.shape
    modes = scaled.shape[0]
    part = pl.BlockSpec((None, modes, plane), lambda p: (p, 0, 0))
    return pl.pallas_call(
        functools.partial(carry_kernel, steps),
        grid=(depth,),
        in_specs=[pl.BlockSpec(memory_space=pltpu.SMEM), part, part],
        out_specs=part,
        out_shape=jax.ShapeDtypeStruct((depth, modes, plane), jnp.float32),
        cost_estimate=SHORT,
        name="carried",
    )(scaled, sums, later)


def fill_tables(steps, aways, scaled, mode_gain, scaled_row, gain_row, table):
    near_weights = caputo_weights()
    modes = scaled.shape[0]

    def lags(columns, ahead):
        row = lax.broadcasted_iota(jnp.int32, (steps, columns), 0)
        return lax.broadcasted_iota(jnp.int32, (steps, columns), 1) - row + ahead

    def far_of(lag):
        distance = jnp.maximum(lag, 0).astype(jnp.float32)
        far = jnp.zeros(lag.shape, jnp.float32)
        for j in range(modes):
            far = far + mode_gain[j] * jnp.exp(-scaled[j] * distance)
        return far

    def near_of(lag):
        near = jnp.zeros(lag.shape, jnp.float32)
        for k, weight in enumerate(near_weights):
            near = jnp.where(lag == k, weight, near)
        return near

    lag = lags(steps, 0)
    table[:, :steps] = jnp.where(lag >= BAND, far_of(lag), near_of(lag))
    lag = lags(BAND, steps)
    table[:, steps : steps + BAND] = jnp.where(lag < BAND, near_of(lag) - far_of(lag), 0.0)
    row = lax.broadcasted_iota(jnp.int32, (steps, modes), 0)
    for k, away in enumerate(aways):
        at = steps + BAND + k * modes
        distance = (away * steps - row).astype(jnp.float32)
        table[:, at : at + modes] = gain_row[...] * jnp.exp(-scaled_row[...] * distance)


def history_kernel(aways, scaled, mode_gain, scaled_row, gain_row, field, *refs):
    parts, (before, image, table, stacked) = refs[: 1 + len(aways)], refs[1 + len(aways) :]
    steps = field.shape[0]

    @pl.when((pl.program_id(0) == 0) & (pl.program_id(1) == 0))
    def _():
        fill_tables(steps, aways, scaled, mode_gain, scaled_row, gain_row, table)

    stacked[:steps, :] = field[...]
    at = steps
    for part in parts:
        stacked[at : at + part.shape[0], :] = part[...]
        at += part.shape[0]
    image[...] = before[...] + dot(table[...], stacked[...])


def add_history(scaled, mode_gain, field, head, aways, later, image):
    depth, steps, plane = field.shape
    modes = scaled.shape[0]
    tile = tile_of(plane)
    operands = (field, head, *later)
    rows = sum(array.shape[1] for array in operands)
    smem = pl.BlockSpec(memory_space=pltpu.SMEM)
    whole = pl.BlockSpec((1, modes), lambda p, c: (0, 0))
    part = lambda p, c: (p, 0, c)
    return pl.pallas_call(
        functools.partial(history_kernel, aways),
        grid=(depth, plane // tile),
        in_specs=[
            smem,
            smem,
            whole,
            whole,
            *[pl.BlockSpec((None, array.shape[1], tile), part) for array in (*operands, image)],
        ],
        out_specs=pl.BlockSpec((None, steps, tile), part),
        out_shape=jax.ShapeDtypeStruct(field.shape, jnp.float32),
        input_output_aliases={4 + len(operands): 0},
        scratch_shapes=[pltpu.VMEM((steps, rows), jnp.float32), pltpu.VMEM((rows, tile), jnp.float32)],
        compiler_params=pltpu.CompilerParams(vmem_limit_bytes=VMEM_LIMIT),
        cost_estimate=SHORT,
        name="add_history",
    )(scaled, mode_gain, scaled[None], mode_gain[None], *operands, image)


def copy_rows(source, out, held, sems):
    pieces = [pl.ds(k * ROWS, ROWS) for k in range(out.shape[0] // ROWS)]
    inward = [
        pltpu.make_async_copy(source.at[rows], held.at[rows], sems.at[0, k]) for k, rows in enumerate(pieces)
    ]
    outward = [
        pltpu.make_async_copy(held.at[rows], out.at[rows], sems.at[1, k]) for k, rows in enumerate(pieces)
    ]
    for copy in inward:
        copy.start()
    for copy, onward in zip(inward, outward):
        copy.wait()
        onward.start()
    for copy in outward:
        copy.wait()


def staged(kernel, name, shape, device, *arrays):
    return pl.pallas_call(
        kernel,
        in_specs=[pl.BlockSpec(memory_space=pltpu.SMEM)] * len(device)
        + [pl.BlockSpec(memory_space=pl.ANY)] * len(arrays),
        out_specs=pl.BlockSpec(memory_space=pl.ANY),
        out_shape=jax.ShapeDtypeStruct(shape, jnp.float32),
        scratch_shapes=[
            pltpu.VMEM(shape, jnp.float32),
            pltpu.SemaphoreType.DMA((2, math.prod(shape[:-1]) // ROWS)),
        ],
        compiler_params=pltpu.CompilerParams(vmem_limit_bytes=VMEM_LIMIT),
        cost_estimate=SHORT,
        name=name,
    )(*device, *arrays)


def rows_kernel(which, lo, device, field, out, held, sems):
    copy_rows(field.at[device[which], pl.ds(lo, out.shape[0])], out, held, sems)


def middle_kernel(lo, field, *refs):
    out, held, sems = refs[-3:]
    copy_rows(field.at[1, pl.ds(lo, out.shape[0])], out, held, sems)


def middle_rows(field, lo, hi, *token):
    kernel = functools.partial(middle_kernel, lo)
    return staged(kernel, "middle_rows", (hi - lo, field.shape[-1]), [], field, *token)


def rows_of(device, which, field, lo, hi):
    kernel = functools.partial(rows_kernel, which, lo)
    return staged(kernel, "rows_of", (hi - lo, field.shape[-1]), [device], field)


def pick_kernel(last, relayed_lo, own_lo, device, field, relayed, out, held, sems):
    count = out.shape[0]

    @pl.when(device[RANK] < last)
    def _():
        copy_rows(relayed.at[pl.ds(relayed_lo, count)], out, held, sems)

    @pl.when(device[RANK] >= last)
    def _():
        copy_rows(field.at[device[OUTER], pl.ds(own_lo, count)], out, held, sems)


def picked_rows(device, field, relayed, last, relayed_lo, own_lo, count):
    kernel = functools.partial(pick_kernel, last, relayed_lo, own_lo)
    return staged(kernel, "picked_rows", (count, field.shape[-1]), [device], field, relayed)


def head_kernel(field, out, held, sems):
    per_plane = BAND // ROWS
    for p in range(out.shape[0]):
        copy_rows(field.at[p, pl.ds(0, BAND)], out.at[p], held.at[p], sems.at[:, pl.ds(p * per_plane, per_plane)])


def head_of(field):
    depth, _, plane = field.shape
    return staged(head_kernel, "head_of", (depth, BAND, plane), [], field)


def join_kernel(*refs):
    arrays, (out, held, sems) = refs[:-3], refs[-3:]
    at = 0
    for array in arrays:
        rows = pl.ds(at, array.shape[0])
        copy_rows(array, out.at[rows], held.at[rows], sems.at[:, pl.ds(at // ROWS, array.shape[0] // ROWS)])
        at += array.shape[0]


def joined(arrays):
    shape = (sum(array.shape[0] for array in arrays), arrays[0].shape[1])
    return staged(join_kernel, "joined", shape, [], *arrays)


def plane_kernel(depth, shifts, absorption, field, *refs):
    image, masks = refs[-2:]
    plane = field.shape[-1]

    @pl.when(pl.program_id(0) == 0)
    def _():
        column = lax.broadcasted_iota(jnp.int32, (1, plane), 1)
        row_pos = column % NY
        for at, offset in enumerate(OFFSETS):
            weight = -DIFFUSION * STENCIL[offset + 2]
            moved = row_pos + offset
            masks[at : at + 1, :] = jnp.where((moved >= 0) & (moved < NY), weight, 0.0)
            at += len(OFFSETS)
            moved = column + offset * NY
            masks[at : at + 1, :] = jnp.where((moved >= 0) & (moved < plane), weight, 0.0)

    for p in range(depth):
        cells = field[p]
        total = (absorption[p][None, :] - 3.0 * DIFFUSION * STENCIL[2]) * cells
        for row, shift in enumerate(shifts):
            total = total + masks[row][None, :] * pltpu.roll(cells, (-shift) % plane, 1)
        for offset in OFFSETS:
            if 0 <= p + offset < depth:
                total = total + (-DIFFUSION * STENCIL[offset + 2]) * field[p + offset]
        image[p] = total


def plane_terms(absorption, field, image, start, end):
    depth, _, plane = field.shape
    shifts = tuple(OFFSETS) + tuple(offset * NY for offset in OFFSETS)
    first = start // ROWS
    slab = pl.BlockSpec((depth, ROWS, plane), lambda t: (0, first + t, 0))
    in_any = pl.BlockSpec(memory_space=pl.ANY)
    started = [] if image is None else [image]
    return pl.pallas_call(
        functools.partial(plane_kernel, depth, shifts),
        grid=((end - start) // ROWS,),
        in_specs=[pl.BlockSpec(absorption.shape, lambda t: (0, 0)), slab] + [in_any] * len(started),
        out_specs=slab,
        scratch_shapes=[pltpu.VMEM((len(shifts), plane), jnp.float32)],
        out_shape=jax.ShapeDtypeStruct(field.shape, jnp.float32),
        input_output_aliases={2: 0} if started else {},
        compiler_params=pltpu.CompilerParams(vmem_limit_bytes=VMEM_LIMIT),
        cost_estimate=SHORT,
        name="plane_terms",
    )(absorption, field, *started)


def update_kernel(change, planes_of, count, start, *refs):
    pieces = count // ROWS
    device, refs = refs[0], refs[1:]
    arrays, (image, held, came, in_sems, came_sems, out_sems) = refs[:-6], refs[-6:]
    beside, before = arrays[: len(change.firsts)], arrays[len(change.firsts)]
    planes = planes_of(device)

    def held_copy(p, k, out):
        there = pl.ds(start + k * ROWS, ROWS)
        here = held.at[p, pl.ds(k * ROWS, ROWS)]
        if out:
            return pltpu.make_async_copy(here, image.at[planes[p], there], out_sems.at[p, k])
        return pltpu.make_async_copy(before.at[planes[p], there], here, in_sems.at[p, k])

    def came_copy(i, k):
        source = beside[i].at[pl.ds(firsts[i] + k * ROWS, ROWS)]
        return pltpu.make_async_copy(source, came.at[i, pl.ds(k * ROWS, ROWS)], came_sems.at[i, k])

    firsts = change.firsts
    for k in range(pieces):
        for i in range(len(beside)):
            came_copy(i, k).start()
        for p in range(len(planes)):
            held_copy(p, k, False).start()
    for k in range(pieces):
        for i in range(len(beside)):
            came_copy(i, k).wait()
        for p in range(len(planes)):
            held_copy(p, k, False).wait()
        at = slice(k * ROWS, (k + 1) * ROWS)
        for p, added in enumerate(change(device, [came[i, at] for i in range(len(beside))])):
            held[p, at] += added
            held_copy(p, k, True).start()
    for k in range(pieces):
        for p in range(len(planes)):
            held_copy(p, k, True).wait()


class Change:
    def __init__(self, change, firsts):
        self.change, self.firsts = change, firsts

    def __call__(self, device, beside):
        return self.change(device, beside)


def update(name, change, planes_of, plane_count, device, arrays, image, start, count, token=()):
    plane = image.shape[-1]
    pieces = count // ROWS
    in_any = pl.BlockSpec(memory_space=pl.ANY)
    return pl.pallas_call(
        functools.partial(update_kernel, Change(change, [row for _, row in arrays]), planes_of, count, start),
        in_specs=[pl.BlockSpec(memory_space=pltpu.SMEM)] + [in_any] * (len(arrays) + 1 + len(token)),
        out_specs=in_any,
        out_shape=jax.ShapeDtypeStruct(image.shape, jnp.float32),
        scratch_shapes=[
            pltpu.VMEM((plane_count, count, plane), jnp.float32),
            pltpu.VMEM((len(arrays), count, plane), jnp.float32),
            pltpu.SemaphoreType.DMA((plane_count, pieces)),
            pltpu.SemaphoreType.DMA((len(arrays), pieces)),
            pltpu.SemaphoreType.DMA((plane_count, pieces)),
        ],
        input_output_aliases={1 + len(arrays): 0},
        compiler_params=pltpu.CompilerParams(vmem_limit_bytes=VMEM_LIMIT),
        cost_estimate=SHORT,
        name=name,
    )(device, *[array for array, _ in arrays], image, *token)


def add_halo(device, near, out_side, over_y, over_z, image, last, start, end):

    def change(device, beside):
        near, out_side, over_y, over_z = beside
        beyond = jnp.where(device[PARTNER_RANK] < last, over_y, over_z)
        return NEAR * beyond + FAR * out_side, FAR * beyond, FAR * near

    def planes_of(device):
        return device[OUTER], device[MIDDLE], device[INNER]

    arrays = (near, out_side, over_y, over_z)
    return update("add_halo", change, planes_of, 3, device, arrays, image, start, end - start)


def add_inner(device, beside, image, start, token):

    def change(device, beside):
        return NEAR * beside[0], FAR * beside[0]

    def planes_of(device):
        return device[INNER], device[MIDDLE]

    return update("add_inner", change, planes_of, 2, device, [(beside, 0)], image, start, beside.shape[0], token)


def cuts(steps, pieces):
    marks = [ROWS * round(steps * i / pieces / ROWS) for i in range(pieces + 1)]
    return list(zip(marks[:-1], marks[1:]))


class Order:
    def __init__(self, token):
        self.token = token

    def __call__(self, value):
        value, self.token = lax.optimization_barrier((value, self.token))
        return value


def per_device(adjoint_field, absorption, mode_rates, mode_weights):
    steps, depth, plane = adjoint_field.shape
    groups = lax.axis_size("tm")
    slabs = lax.axis_size("space")
    pairs = slabs // 2
    me = lax.axis_index("space")
    odd = me % 2
    field = adjoint_field.transpose(1, 0, 2)
    order = Order(mode_rates)

    swap = [(i, i ^ 1) for i in range(slabs)]
    outward = [(i, i - 2 if i % 2 == 0 else i + 2) for i in range(slabs)]
    outward = [(a, b) for a, b in outward if 0 <= b < slabs]
    onward = [(i, i + 2 if i % 2 == 0 else i - 2) for i in range(slabs)]
    onward = [(a, b) for a, b in onward if 0 <= b < slabs]

    def back(distance):
        return [(i, i - distance) for i in range(distance, groups)]


    def rank(i):
        return i // 2 if i % 2 == 0 else pairs - 1 - i // 2

    device = jnp.stack(
        [
            jnp.where(odd == 0, 0, depth - 1),
            jnp.where(odd == 0, depth - 1, 0),
            jnp.where(odd == 0, depth - 2, 1),
            jnp.where(odd == 0, me // 2, pairs - 1 - me // 2),
            jnp.where(odd == 1, me // 2, pairs - 1 - me // 2),
        ]
    ).astype(jnp.int32)

    def send(value, axis, route):
        return lax.ppermute(order(value), axis, route)

    def whole_rows(share):
        return ROWS * round(steps * share / ROWS)

    def between(*marks):
        return list(zip(marks[:-1], marks[1:]))

    mid_cuts = between(0, whole_rows(1 / 2), steps)
    out_cuts = cuts(steps, pairs)
    in_cuts = between(0, whole_rows(9 / 16), steps - ROWS, steps)
    plane_cuts = cuts(steps, 4)
    slots = pairs - 1

    def middle_send(k):
        token = [order.token] if k else []
        return send(middle_rows(field, *mid_cuts[k], *token), "space", swap)

    def outer_send(j):
        last = slots - j
        lo, hi = out_cuts[j]
        own_lo, own_hi = out_cuts[j + 1]
        first = out_cuts[(slots + 1) // 2][0]
        got, at = (relayed[0], lo) if lo < first else (relayed[1], lo - first)
        return send(
            picked_rows(order(device), field, got, last, at, own_lo, own_hi - own_lo), "space", swap
        )

    def outer_onward(parts):
        route = [(a, b) for a, b in onward if parts[-1] >= slots - rank(a ^ 1)]
        return send(y_out[parts[0]] if len(parts) == 1 else together, "space", route)

    def inner_send(k):
        return send(rows_of(order(device), INNER, field, *in_cuts[k]), "space", swap)

    def relay(lo, hi):
        return send(rows_of(order(device), OUTER, field, lo, hi), "space", outward)

    y_steps = [functools.partial(middle_send, k) for k in range(len(mid_cuts))]
    y_steps += [functools.partial(outer_send, j) for j in range(slots)]
    y_steps += [functools.partial(inner_send, k) for k in range(len(in_cuts))]
    sent = []

    def next_y():
        if len(sent) < len(y_steps):
            sent.append(y_steps[len(sent)]())

    scaled, mode_gain = mode_tables(mode_rates, mode_weights, steps * groups)
    next_y()
    next_y()
    first = out_cuts[(slots + 1) // 2][0]
    relayed = [relay(0, first)]
    head = send(head_of(order(field)), "tm", back(1))
    sums = mode_sums(order(scaled), field)
    aways = [1]
    later = [send(sums, "tm", back(1))]

    def plane(k, image):
        return order(plane_terms(order(absorption), field, image, *plane_cuts[k]))

    image = plane(0, None)
    y_mid = [order(sent[0])]
    z_mid = [send(y_mid[0], "space", onward)]
    relayed[0] = order(relayed[0])
    next_y()
    head = order(head)
    later[0] = order(later[0])
    if first < out_cuts[slots][0]:
        relayed.append(relay(first, out_cuts[slots][0]))
    while 2 * aways[-1] < groups:
        if len(aways) > 1:
            later[-1] = order(later[-1])
        sums = carried(order(scaled), aways[-1] * steps, sums, later[-1])
        aways.append(2 * aways[-1])
        later.append(send(sums, "tm", back(aways[-1])))

    image = plane(1, image)
    y_mid.append(order(sent[1]))
    next_y()
    image = plane(2, image)

    def halo(q, image):
        lo, hi = out_cuts[q]
        over_z = y_out[0] if q == 0 else z_last if q == slots else z_most
        at_z = out_cuts[q - 1][0] if 0 < q < slots else 0
        over_y = (y_out[q], 0) if q < slots else (over_z, 0)
        if q == 0:
            over_z = jnp.zeros_like(over_z)
        for k, (start, end) in enumerate(mid_cuts):
            a, b = max(lo, start), min(hi, end)
            if a < b:
                image = add_halo(
                    order(device), (y_mid[k], a - start), (z_mid[k], a - start), (over_y[0], a - lo),
                    (over_z, at_z + a - lo), image, slots - q, a, b,
                )
        return order(image)

    y_out = []
    def inner(k, image):
        token = [order.token] if k == len(in_cuts) - 1 else []
        return order(add_inner(order(device), y_in[k], image, in_cuts[k][0], token))

    for j in range(slots):
        y_out.append(order(sent[2 + j]))
        if j == 0:
            relayed[1:] = order(relayed[1:])
        if j < slots - 1:
            next_y()
        if j == 0:
            z_mid.append(send(y_mid[1], "space", onward))
            image = plane(3, image)
        if j == min(1, slots - 1):
            later[1:] = order(later[1:])
        if j == slots - 2:
            together = joined(order(list(y_out)))
    z_mid[0] = order(z_mid[0])
    most = list(range(slots - 1))
    z_most = outer_onward(most) if most else None
    next_y()
    z_mid[1] = order(z_mid[1])
    z_last = outer_onward([slots - 1])
    image = halo(0, image)
    image = order(add_history(order(scaled), mode_gain, field, head, aways, later, image))
    y_in = [order(sent[2 + slots])]
    next_y()
    image = inner(0, image)
    if most:
        z_most = order(z_most)
    for q in range(1, slots):
        image = halo(q, image)
    z_last = order(z_last)
    image = halo(slots, image)
    for k in range(1, len(in_cuts)):
        y_in.append(order(sent[2 + slots + k]))
        image = inner(k, image)
    return image.transpose(1, 0, 2)


def solution(mesh):
    return jax.shard_map(
        per_device,
        mesh=mesh,
        in_specs=(P("tm", "space", None), P("space", None), P(), P()),
        out_specs=P("tm", "space", None),
        check_vma=False,
    )
```

```python
import functools
import math

import jax
import jax.numpy as jnp
from jax import lax
from jax.experimental import pallas as pl
from jax.experimental.pallas import tpu as pltpu
from jax.sharding import PartitionSpec as P
import numpy as np

NY = 96
BAND = 16

DIFFUSION = 0.2
ORDER_EXP = 0.4
STENCIL = (-1.0 / 12.0, 16.0 / 12.0, -30.0 / 12.0, 16.0 / 12.0, -1.0 / 12.0)
NEAR = -DIFFUSION * STENCIL[1]
FAR = -DIFFUSION * STENCIL[0]
OFFSETS = (-2, -1, 1, 2)
ROWS = 8
VMEM_LIMIT = 48 * 1024 * 1024
SHORT = pl.CostEstimate(flops=1, bytes_accessed=1, transcendentals=0)

OUTER, INNER, MIDDLE, RANK, PARTNER_RANK = range(5)


def mode_tables(mode_rates, mode_weights, total_steps):
    scaled = mode_rates / total_steps
    mode_gain = mode_weights * jnp.sqrt(-jnp.expm1(-2.0 * scaled))
    return scaled, mode_gain


def caputo_weights():
    grown = np.arange(BAND + 1, dtype=np.float64) ** ORDER_EXP
    increments = grown[1:] - grown[:-1]
    return [float(w) for w in np.diff(increments, prepend=0.0)]


def dot(a, b):
    return jnp.dot(a, b, precision=lax.Precision.HIGHEST, preferred_element_type=jnp.float32)


def tile_of(plane):
    for count in range(4, plane + 1):
        if plane % count == 0 and (plane // count) % 128 == 0:
            return plane // count
    return plane


def sums_kernel(scaled, field, sums, projector):
    modes, steps = projector.shape

    @pl.when((pl.program_id(0) == 0) & (pl.program_id(1) == 0))
    def _():
        pos = lax.broadcasted_iota(jnp.int32, (1, steps), 1).astype(jnp.float32)
        for j in range(modes):
            projector[j : j + 1, :] = jnp.exp(-scaled[j] * pos)

    sums[...] = dot(projector[...], field[...])


def mode_sums(scaled, field):
    depth, steps, plane = field.shape
    modes = scaled.shape[0]
    tile = tile_of(plane)
    return pl.pallas_call(
        sums_kernel,
        grid=(depth, plane // tile),
        in_specs=[
            pl.BlockSpec(memory_space=pltpu.SMEM),
            pl.BlockSpec((None, steps, tile), lambda p, c: (p, 0, c)),
        ],
        out_specs=pl.BlockSpec((None, modes, tile), lambda p, c: (p, 0, c)),
        out_shape=jax.ShapeDtypeStruct((depth, modes, plane), jnp.float32),
        scratch_shapes=[pltpu.VMEM((modes, steps), jnp.float32)],
        compiler_params=pltpu.CompilerParams(vmem_limit_bytes=VMEM_LIMIT),
        cost_estimate=SHORT,
        name="mode_sums",
    )(scaled, field)


def carry_kernel(steps, scaled, sums, later, total):
    for j in range(total.shape[0]):
        decay = jnp.exp(jnp.full((1, total.shape[1]), -scaled[j] * steps, jnp.float32))
        total[j : j + 1, :] = sums[j : j + 1, :] + decay * later[j : j + 1, :]


def carried(scaled, steps, sums, later):
    depth, _, plane = sums.shape
    modes = scaled.shape[0]
    part = pl.BlockSpec((None, modes, plane), lambda p: (p, 0, 0))
    return pl.pallas_call(
        functools.partial(carry_kernel, steps),
        grid=(depth,),
        in_specs=[pl.BlockSpec(memory_space=pltpu.SMEM), part, part],
        out_specs=part,
        out_shape=jax.ShapeDtypeStruct((depth, modes, plane), jnp.float32),
        cost_estimate=SHORT,
        name="carried",
    )(scaled, sums, later)


def fill_tables(steps, aways, scaled, mode_gain, scaled_row, gain_row, table):
    near_weights = caputo_weights()
    modes = scaled.shape[0]

    def lags(columns, ahead):
        row = lax.broadcasted_iota(jnp.int32, (steps, columns), 0)
        return lax.broadcasted_iota(jnp.int32, (steps, columns), 1) - row + ahead

    def far_of(lag):
        distance = jnp.maximum(lag, 0).astype(jnp.float32)
        far = jnp.zeros(lag.shape, jnp.float32)
        for j in range(modes):
            far = far + mode_gain[j] * jnp.exp(-scaled[j] * distance)
        return far

    def near_of(lag):
        near = jnp.zeros(lag.shape, jnp.float32)
        for k, weight in enumerate(near_weights):
            near = jnp.where(lag == k, weight, near)
        return near

    lag = lags(steps, 0)
    table[:, :steps] = jnp.where(lag >= BAND, far_of(lag), near_of(lag))
    lag = lags(BAND, steps)
    table[:, steps : steps + BAND] = jnp.where(lag < BAND, near_of(lag) - far_of(lag), 0.0)
    row = lax.broadcasted_iota(jnp.int32, (steps, modes), 0)
    for k, away in enumerate(aways):
        at = steps + BAND + k * modes
        distance = (away * steps - row).astype(jnp.float32)
        table[:, at : at + modes] = gain_row[...] * jnp.exp(-scaled_row[...] * distance)


def history_kernel(aways, scaled, mode_gain, scaled_row, gain_row, field, *refs):
    parts, (before, image, table, stacked) = refs[: 1 + len(aways)], refs[1 + len(aways) :]
    steps = field.shape[0]

    @pl.when((pl.program_id(0) == 0) & (pl.program_id(1) == 0))
    def _():
        fill_tables(steps, aways, scaled, mode_gain, scaled_row, gain_row, table)

    stacked[:steps, :] = field[...]
    at = steps
    for part in parts:
        stacked[at : at + part.shape[0], :] = part[...]
        at += part.shape[0]
    image[...] = before[...] + dot(table[...], stacked[...])


def add_history(scaled, mode_gain, field, head, aways, later, image):
    depth, steps, plane = field.shape
    modes = scaled.shape[0]
    tile = tile_of(plane)
    operands = (field, head, *later)
    rows = sum(array.shape[1] for array in operands)
    smem = pl.BlockSpec(memory_space=pltpu.SMEM)
    whole = pl.BlockSpec((1, modes), lambda p, c: (0, 0))
    part = lambda p, c: (p, 0, c)
    return pl.pallas_call(
        functools.partial(history_kernel, aways),
        grid=(depth, plane // tile),
        in_specs=[
            smem,
            smem,
            whole,
            whole,
            *[pl.BlockSpec((None, array.shape[1], tile), part) for array in (*operands, image)],
        ],
        out_specs=pl.BlockSpec((None, steps, tile), part),
        out_shape=jax.ShapeDtypeStruct(field.shape, jnp.float32),
        input_output_aliases={4 + len(operands): 0},
        scratch_shapes=[pltpu.VMEM((steps, rows), jnp.float32), pltpu.VMEM((rows, tile), jnp.float32)],
        compiler_params=pltpu.CompilerParams(vmem_limit_bytes=VMEM_LIMIT),
        cost_estimate=SHORT,
        name="add_history",
    )(scaled, mode_gain, scaled[None], mode_gain[None], *operands, image)


def copy_rows(source, out, held, sems):
    pieces = [pl.ds(k * ROWS, ROWS) for k in range(out.shape[0] // ROWS)]
    inward = [
        pltpu.make_async_copy(source.at[rows], held.at[rows], sems.at[0, k]) for k, rows in enumerate(pieces)
    ]
    outward = [
        pltpu.make_async_copy(held.at[rows], out.at[rows], sems.at[1, k]) for k, rows in enumerate(pieces)
    ]
    for copy in inward:
        copy.start()
    for copy, onward in zip(inward, outward):
        copy.wait()
        onward.start()
    for copy in outward:
        copy.wait()


def staged(kernel, name, shape, device, *arrays):
    return pl.pallas_call(
        kernel,
        in_specs=[pl.BlockSpec(memory_space=pltpu.SMEM)] * len(device)
        + [pl.BlockSpec(memory_space=pl.ANY)] * len(arrays),
        out_specs=pl.BlockSpec(memory_space=pl.ANY),
        out_shape=jax.ShapeDtypeStruct(shape, jnp.float32),
        scratch_shapes=[
            pltpu.VMEM(shape, jnp.float32),
            pltpu.SemaphoreType.DMA((2, math.prod(shape[:-1]) // ROWS)),
        ],
        compiler_params=pltpu.CompilerParams(vmem_limit_bytes=VMEM_LIMIT),
        cost_estimate=SHORT,
        name=name,
    )(*device, *arrays)


def place_of(me, slabs, depth):
    odd = me % 2
    half = me // 2
    back = slabs // 2 - 1 - half
    return [
        jnp.where(odd == 0, 0, depth - 1),
        jnp.where(odd == 0, depth - 1, 0),
        jnp.where(odd == 0, depth - 2, 1),
        jnp.where(odd == 0, half, back),
        jnp.where(odd == 1, half, back),
    ]


def rows_kernel(which, lo, device, field, out, held, sems):
    copy_rows(field.at[device[which], pl.ds(lo, out.shape[0])], out, held, sems)


def middle_kernel(lo, field, *refs):
    out, held, sems = refs[-3:]
    copy_rows(field.at[1, pl.ds(lo, out.shape[0])], out, held, sems)


def middle_rows(field, lo, hi, *token):
    kernel = functools.partial(middle_kernel, lo)
    return staged(kernel, "middle_rows", (hi - lo, field.shape[-1]), [], field, *token)


def rows_of(device, which, field, lo, hi):
    kernel = functools.partial(rows_kernel, which, lo)
    return staged(kernel, "rows_of", (hi - lo, field.shape[-1]), [device], field)


def pick_kernel(last, relayed_lo, own_lo, device, field, relayed, out, held, sems):
    count = out.shape[0]

    @pl.when(device[RANK] < last)
    def _():
        copy_rows(relayed.at[pl.ds(relayed_lo, count)], out, held, sems)

    @pl.when(device[RANK] >= last)
    def _():
        copy_rows(field.at[device[OUTER], pl.ds(own_lo, count)], out, held, sems)


def picked_rows(device, field, relayed, last, relayed_lo, own_lo, count):
    kernel = functools.partial(pick_kernel, last, relayed_lo, own_lo)
    return staged(kernel, "picked_rows", (count, field.shape[-1]), [device], field, relayed)


def head_kernel(field, out, held, sems):
    per_plane = BAND // ROWS
    for p in range(out.shape[0]):
        copy_rows(field.at[p, pl.ds(0, BAND)], out.at[p], held.at[p], sems.at[:, pl.ds(p * per_plane, per_plane)])


def head_of(field):
    depth, _, plane = field.shape
    return staged(head_kernel, "head_of", (depth, BAND, plane), [], field)


def join_kernel(*refs):
    arrays, (out, held, sems) = refs[:-3], refs[-3:]
    at = 0
    for array in arrays:
        rows = pl.ds(at, array.shape[0])
        copy_rows(array, out.at[rows], held.at[rows], sems.at[:, pl.ds(at // ROWS, array.shape[0] // ROWS)])
        at += array.shape[0]


def joined(arrays):
    shape = (sum(array.shape[0] for array in arrays), arrays[0].shape[1])
    return staged(join_kernel, "joined", shape, [], *arrays)


def plane_kernel(depth, shifts, absorption, field, *refs):
    image, masks = refs[-2:]
    plane = field.shape[-1]

    @pl.when(pl.program_id(0) == 0)
    def _():
        column = lax.broadcasted_iota(jnp.int32, (1, plane), 1)
        row_pos = column % NY
        for at, offset in enumerate(OFFSETS):
            weight = -DIFFUSION * STENCIL[offset + 2]
            moved = row_pos + offset
            masks[at : at + 1, :] = jnp.where((moved >= 0) & (moved < NY), weight, 0.0)
            at += len(OFFSETS)
            moved = column + offset * NY
            masks[at : at + 1, :] = jnp.where((moved >= 0) & (moved < plane), weight, 0.0)

    for p in range(depth):
        cells = field[p]
        total = (absorption[p][None, :] - 3.0 * DIFFUSION * STENCIL[2]) * cells
        for row, shift in enumerate(shifts):
            total = total + masks[row][None, :] * pltpu.roll(cells, (-shift) % plane, 1)
        for offset in OFFSETS:
            if 0 <= p + offset < depth:
                total = total + (-DIFFUSION * STENCIL[offset + 2]) * field[p + offset]
        image[p] = total


def plane_terms(absorption, field, image, start, end):
    depth, _, plane = field.shape
    shifts = tuple(OFFSETS) + tuple(offset * NY for offset in OFFSETS)
    first = start // ROWS
    slab = pl.BlockSpec((depth, ROWS, plane), lambda t: (0, first + t, 0))
    in_any = pl.BlockSpec(memory_space=pl.ANY)
    started = [] if image is None else [image]
    return pl.pallas_call(
        functools.partial(plane_kernel, depth, shifts),
        grid=((end - start) // ROWS,),
        in_specs=[pl.BlockSpec(absorption.shape, lambda t: (0, 0)), slab] + [in_any] * len(started),
        out_specs=slab,
        scratch_shapes=[pltpu.VMEM((len(shifts), plane), jnp.float32)],
        out_shape=jax.ShapeDtypeStruct(field.shape, jnp.float32),
        input_output_aliases={2: 0} if started else {},
        compiler_params=pltpu.CompilerParams(vmem_limit_bytes=VMEM_LIMIT),
        cost_estimate=SHORT,
        name="plane_terms",
    )(absorption, field, *started)


def update_kernel(change, planes_of, count, start, *refs):
    pieces = count // ROWS
    arrays, (image, held, came, in_sems, came_sems, out_sems) = refs[:-6], refs[-6:]
    beside, before = arrays[: len(change.firsts)], arrays[len(change.firsts)]
    device = place_of(lax.axis_index("space"), lax.axis_size("space"), image.shape[0])
    planes = planes_of(device)

    def held_copy(p, k, out):
        there = pl.ds(start + k * ROWS, ROWS)
        here = held.at[p, pl.ds(k * ROWS, ROWS)]
        if out:
            return pltpu.make_async_copy(here, image.at[planes[p], there], out_sems.at[p, k])
        return pltpu.make_async_copy(before.at[planes[p], there], here, in_sems.at[p, k])

    def came_copy(i, k):
        source = beside[i].at[pl.ds(firsts[i] + k * ROWS, ROWS)]
        return pltpu.make_async_copy(source, came.at[i, pl.ds(k * ROWS, ROWS)], came_sems.at[i, k])

    firsts = change.firsts
    for k in range(pieces):
        for i in range(len(beside)):
            came_copy(i, k).start()
        for p in range(len(planes)):
            held_copy(p, k, False).start()
    for k in range(pieces):
        for i in range(len(beside)):
            came_copy(i, k).wait()
        for p in range(len(planes)):
            held_copy(p, k, False).wait()
        at = slice(k * ROWS, (k + 1) * ROWS)
        for p, added in enumerate(change(device, [came[i, at] for i in range(len(beside))])):
            held[p, at] += added
            held_copy(p, k, True).start()
    for k in range(pieces):
        for p in range(len(planes)):
            held_copy(p, k, True).wait()


class Change:
    def __init__(self, change, firsts):
        self.change, self.firsts = change, firsts

    def __call__(self, device, beside):
        return self.change(device, beside)


def update(name, change, planes_of, plane_count, arrays, image, start, count, token=()):
    plane = image.shape[-1]
    pieces = count // ROWS
    in_any = pl.BlockSpec(memory_space=pl.ANY)
    return pl.pallas_call(
        functools.partial(update_kernel, Change(change, [row for _, row in arrays]), planes_of, count, start),
        in_specs=[in_any] * (len(arrays) + 1 + len(token)),
        out_specs=in_any,
        out_shape=jax.ShapeDtypeStruct(image.shape, jnp.float32),
        scratch_shapes=[
            pltpu.VMEM((plane_count, count, plane), jnp.float32),
            pltpu.VMEM((len(arrays), count, plane), jnp.float32),
            pltpu.SemaphoreType.DMA((plane_count, pieces)),
            pltpu.SemaphoreType.DMA((len(arrays), pieces)),
            pltpu.SemaphoreType.DMA((plane_count, pieces)),
        ],
        input_output_aliases={len(arrays): 0},
        compiler_params=pltpu.CompilerParams(vmem_limit_bytes=VMEM_LIMIT),
        cost_estimate=SHORT,
        name=name,
    )(*[array for array, _ in arrays], image, *token)


def add_halo(near, out_side, over_y, over_z, image, last, start, end):

    def change(device, beside):
        near, out_side, over_y, over_z = beside
        beyond = jnp.where(device[PARTNER_RANK] < last, over_y, over_z)
        return NEAR * beyond + FAR * out_side, FAR * beyond, FAR * near

    def planes_of(device):
        return device[OUTER], device[MIDDLE], device[INNER]

    arrays = (near, out_side, over_y, over_z)
    return update("add_halo", change, planes_of, 3, arrays, image, start, end - start)


def add_inner(beside, image, start, token):

    def change(device, beside):
        return NEAR * beside[0], FAR * beside[0]

    def planes_of(device):
        return device[INNER], device[MIDDLE]

    return update("add_inner", change, planes_of, 2, [(beside, 0)], image, start, beside.shape[0], token)


def cuts(steps, pieces):
    marks = [ROWS * round(steps * i / pieces / ROWS) for i in range(pieces + 1)]
    return list(zip(marks[:-1], marks[1:]))


class Order:
    def __init__(self, token):
        self.token = token

    def __call__(self, value):
        value, self.token = lax.optimization_barrier((value, self.token))
        return value


def per_device(adjoint_field, absorption, mode_rates, mode_weights):
    steps, depth, plane = adjoint_field.shape
    groups = lax.axis_size("tm")
    slabs = lax.axis_size("space")
    pairs = slabs // 2
    me = lax.axis_index("space")
    field = adjoint_field.transpose(1, 0, 2)
    order = Order(mode_rates)

    swap = [(i, i ^ 1) for i in range(slabs)]
    outward = [(i, i - 2 if i % 2 == 0 else i + 2) for i in range(slabs)]
    outward = [(a, b) for a, b in outward if 0 <= b < slabs]
    onward = [(i, i + 2 if i % 2 == 0 else i - 2) for i in range(slabs)]
    onward = [(a, b) for a, b in onward if 0 <= b < slabs]

    def back(distance):
        return [(i, i - distance) for i in range(distance, groups)]


    def rank(i):
        return i // 2 if i % 2 == 0 else pairs - 1 - i // 2

    device = jnp.stack(place_of(me, slabs, depth)).astype(jnp.int32)

    def send(value, axis, route):
        return lax.ppermute(order(value), axis, route)

    def whole_rows(share):
        return ROWS * round(steps * share / ROWS)

    def between(*marks):
        return list(zip(marks[:-1], marks[1:]))

    mid_cuts = between(0, whole_rows(1 / 2), steps)
    out_cuts = cuts(steps, pairs)
    in_cuts = between(0, whole_rows(9 / 16), steps - ROWS, steps)
    plane_cuts = cuts(steps, 4)
    slots = pairs - 1

    def middle_send(k):
        token = [order.token] if k else []
        return send(middle_rows(field, *mid_cuts[k], *token), "space", swap)

    def outer_send(j):
        last = slots - j
        lo, hi = out_cuts[j]
        own_lo, own_hi = out_cuts[j + 1]
        first = out_cuts[(slots + 1) // 2][0]
        got, at = (relayed[0], lo) if lo < first else (relayed[1], lo - first)
        return send(
            picked_rows(order(device), field, got, last, at, own_lo, own_hi - own_lo), "space", swap
        )

    def outer_onward(parts):
        route = [(a, b) for a, b in onward if parts[-1] >= slots - rank(a ^ 1)]
        return send(y_out[parts[0]] if len(parts) == 1 else together, "space", route)

    def inner_send(k):
        return send(rows_of(order(device), INNER, field, *in_cuts[k]), "space", swap)

    def relay(lo, hi):
        return send(rows_of(order(device), OUTER, field, lo, hi), "space", outward)

    y_steps = [functools.partial(middle_send, k) for k in range(len(mid_cuts))]
    y_steps += [functools.partial(outer_send, j) for j in range(slots)]
    y_steps += [functools.partial(inner_send, k) for k in range(len(in_cuts))]
    sent = []

    def next_y():
        if len(sent) < len(y_steps):
            sent.append(y_steps[len(sent)]())

    scaled, mode_gain = mode_tables(mode_rates, mode_weights, steps * groups)
    next_y()
    next_y()
    first = out_cuts[(slots + 1) // 2][0]
    relayed = [relay(0, first)]
    head = send(head_of(order(field)), "tm", back(1))
    sums = mode_sums(order(scaled), field)
    aways = [1]
    later = [send(sums, "tm", back(1))]

    def plane(k, image):
        return order(plane_terms(order(absorption), field, image, *plane_cuts[k]))

    image = plane(0, None)
    y_mid = [order(sent[0])]
    z_mid = [send(y_mid[0], "space", onward)]
    relayed[0] = order(relayed[0])
    next_y()
    head = order(head)
    later[0] = order(later[0])
    if first < out_cuts[slots][0]:
        relayed.append(relay(first, out_cuts[slots][0]))
    while 2 * aways[-1] < groups:
        if len(aways) > 1:
            later[-1] = order(later[-1])
        sums = carried(order(scaled), aways[-1] * steps, sums, later[-1])
        aways.append(2 * aways[-1])
        later.append(send(sums, "tm", back(aways[-1])))

    image = plane(1, image)
    y_mid.append(order(sent[1]))
    next_y()
    image = plane(2, image)

    def halo(q, image):
        lo, hi = out_cuts[q]
        over_z = y_out[0] if q == 0 else z_last if q == slots else z_most
        at_z = out_cuts[q - 1][0] if 0 < q < slots else 0
        over_y = (y_out[q], 0) if q < slots else (over_z, 0)
        if q == 0:
            over_z = jnp.zeros_like(over_z)
        for k, (start, end) in enumerate(mid_cuts):
            a, b = max(lo, start), min(hi, end)
            if a < b:
                image = add_halo(
                    (y_mid[k], a - start), (z_mid[k], a - start), (over_y[0], a - lo),
                    (over_z, at_z + a - lo), image, slots - q, a, b,
                )
        return order(image)

    y_out = []
    def inner(k, image):
        token = [order.token] if k == len(in_cuts) - 1 else []
        return order(add_inner(y_in[k], image, in_cuts[k][0], token))

    for j in range(slots):
        y_out.append(order(sent[2 + j]))
        if j == 0:
            relayed[1:] = order(relayed[1:])
        if j < slots - 1:
            next_y()
        if j == 0:
            z_mid.append(send(y_mid[1], "space", onward))
            image = plane(3, image)
        if j == min(1, slots - 1):
            later[1:] = order(later[1:])
        if j == slots - 2:
            together = joined(order(list(y_out)))
    z_mid[0] = order(z_mid[0])
    most = list(range(slots - 1))
    z_most = outer_onward(most) if most else None
    next_y()
    z_mid[1] = order(z_mid[1])
    z_last = outer_onward([slots - 1])
    image = halo(0, image)
    image = order(add_history(order(scaled), mode_gain, field, head, aways, later, image))
    y_in = [order(sent[2 + slots])]
    next_y()
    image = inner(0, image)
    if most:
        z_most = order(z_most)
    for q in range(1, slots):
        image = halo(q, image)
    z_last = order(z_last)
    image = halo(slots, image)
    for k in range(1, len(in_cuts)):
        y_in.append(order(sent[2 + slots + k]))
        image = inner(k, image)
    return image.transpose(1, 0, 2)


def solution(mesh):
    return jax.shard_map(
        per_device,
        mesh=mesh,
        in_specs=(P("tm", "space", None), P("space", None), P(), P()),
        out_specs=P("tm", "space", None),
        check_vma=False,
    )
```

```python
import functools
import math

import jax
import jax.numpy as jnp
from jax import lax
from jax.experimental import pallas as pl
from jax.experimental.pallas import tpu as pltpu
from jax.sharding import PartitionSpec as P
import numpy as np

NY = 96
BAND = 16

DIFFUSION = 0.2
ORDER_EXP = 0.4
STENCIL = (-1.0 / 12.0, 16.0 / 12.0, -30.0 / 12.0, 16.0 / 12.0, -1.0 / 12.0)
NEAR = -DIFFUSION * STENCIL[1]
FAR = -DIFFUSION * STENCIL[0]
OFFSETS = (-2, -1, 1, 2)
ROWS = 8
VMEM_LIMIT = 48 * 1024 * 1024
SHORT = pl.CostEstimate(flops=1, bytes_accessed=1, transcendentals=0)

OUTER, INNER, MIDDLE, RANK, PARTNER_RANK = range(5)


def mode_tables(mode_rates, mode_weights, total_steps):
    scaled = mode_rates / total_steps
    mode_gain = mode_weights * jnp.sqrt(-jnp.expm1(-2.0 * scaled))
    return scaled, mode_gain


def caputo_weights():
    grown = np.arange(BAND + 1, dtype=np.float64) ** ORDER_EXP
    increments = grown[1:] - grown[:-1]
    return [float(w) for w in np.diff(increments, prepend=0.0)]


def dot(a, b):
    return jnp.dot(a, b, precision=lax.Precision.HIGHEST, preferred_element_type=jnp.float32)


def tile_of(plane):
    for count in range(4, plane + 1):
        if plane % count == 0 and (plane // count) % 128 == 0:
            return plane // count
    return plane


def sums_kernel(scaled, field, sums, projector):
    modes, steps = projector.shape

    @pl.when((pl.program_id(0) == 0) & (pl.program_id(1) == 0))
    def _():
        pos = lax.broadcasted_iota(jnp.int32, (1, steps), 1).astype(jnp.float32)
        for j in range(modes):
            projector[j : j + 1, :] = jnp.exp(-scaled[j] * pos)

    sums[...] = dot(projector[...], field[...])


def mode_sums(scaled, field):
    depth, steps, plane = field.shape
    modes = scaled.shape[0]
    tile = tile_of(plane)
    return pl.pallas_call(
        sums_kernel,
        grid=(depth, plane // tile),
        in_specs=[
            pl.BlockSpec(memory_space=pltpu.SMEM),
            pl.BlockSpec((None, steps, tile), lambda p, c: (p, 0, c)),
        ],
        out_specs=pl.BlockSpec((None, modes, tile), lambda p, c: (p, 0, c)),
        out_shape=jax.ShapeDtypeStruct((depth, modes, plane), jnp.float32),
        scratch_shapes=[pltpu.VMEM((modes, steps), jnp.float32)],
        compiler_params=pltpu.CompilerParams(vmem_limit_bytes=VMEM_LIMIT),
        cost_estimate=SHORT,
        name="mode_sums",
    )(scaled, field)


def carry_kernel(steps, scaled, sums, later, total):
    for j in range(total.shape[0]):
        decay = jnp.exp(jnp.full((1, total.shape[1]), -scaled[j] * steps, jnp.float32))
        total[j : j + 1, :] = sums[j : j + 1, :] + decay * later[j : j + 1, :]


def carried(scaled, steps, sums, later):
    depth, _, plane = sums.shape
    modes = scaled.shape[0]
    part = pl.BlockSpec((None, modes, plane), lambda p: (p, 0, 0))
    return pl.pallas_call(
        functools.partial(carry_kernel, steps),
        grid=(depth,),
        in_specs=[pl.BlockSpec(memory_space=pltpu.SMEM), part, part],
        out_specs=part,
        out_shape=jax.ShapeDtypeStruct((depth, modes, plane), jnp.float32),
        cost_estimate=SHORT,
        name="carried",
    )(scaled, sums, later)


def fill_tables(steps, aways, scaled, mode_gain, scaled_row, gain_row, table):
    near_weights = caputo_weights()
    modes = scaled.shape[0]

    def lags(columns, ahead):
        row = lax.broadcasted_iota(jnp.int32, (steps, columns), 0)
        return lax.broadcasted_iota(jnp.int32, (steps, columns), 1) - row + ahead

    def far_of(lag):
        distance = jnp.maximum(lag, 0).astype(jnp.float32)
        far = jnp.zeros(lag.shape, jnp.float32)
        for j in range(modes):
            far = far + mode_gain[j] * jnp.exp(-scaled[j] * distance)
        return far

    def near_of(lag):
        near = jnp.zeros(lag.shape, jnp.float32)
        for k, weight in enumerate(near_weights):
            near = jnp.where(lag == k, weight, near)
        return near

    lag = lags(steps, 0)
    table[:, :steps] = jnp.where(lag >= BAND, far_of(lag), near_of(lag))
    lag = lags(BAND, steps)
    table[:, steps : steps + BAND] = jnp.where(lag < BAND, near_of(lag) - far_of(lag), 0.0)
    row = lax.broadcasted_iota(jnp.int32, (steps, modes), 0)
    for k, away in enumerate(aways):
        at = steps + BAND + k * modes
        distance = (away * steps - row).astype(jnp.float32)
        table[:, at : at + modes] = gain_row[...] * jnp.exp(-scaled_row[...] * distance)


def history_kernel(aways, scaled, mode_gain, scaled_row, gain_row, field, *refs):
    parts, (before, image, table, stacked) = refs[: 1 + len(aways)], refs[1 + len(aways) :]
    steps = field.shape[0]

    @pl.when((pl.program_id(0) == 0) & (pl.program_id(1) == 0))
    def _():
        fill_tables(steps, aways, scaled, mode_gain, scaled_row, gain_row, table)

    stacked[:steps, :] = field[...]
    at = steps
    for part in parts:
        stacked[at : at + part.shape[0], :] = part[...]
        at += part.shape[0]
    image[...] = before[...] + dot(table[...], stacked[...])


def add_history(scaled, mode_gain, field, head, aways, later, image):
    depth, steps, plane = field.shape
    modes = scaled.shape[0]
    tile = tile_of(plane)
    operands = (field, head, *later)
    rows = sum(array.shape[1] for array in operands)
    smem = pl.BlockSpec(memory_space=pltpu.SMEM)
    whole = pl.BlockSpec((1, modes), lambda p, c: (0, 0))
    part = lambda p, c: (p, 0, c)
    return pl.pallas_call(
        functools.partial(history_kernel, aways),
        grid=(depth, plane // tile),
        in_specs=[
            smem,
            smem,
            whole,
            whole,
            *[pl.BlockSpec((None, array.shape[1], tile), part) for array in (*operands, image)],
        ],
        out_specs=pl.BlockSpec((None, steps, tile), part),
        out_shape=jax.ShapeDtypeStruct(field.shape, jnp.float32),
        input_output_aliases={4 + len(operands): 0},
        scratch_shapes=[pltpu.VMEM((steps, rows), jnp.float32), pltpu.VMEM((rows, tile), jnp.float32)],
        compiler_params=pltpu.CompilerParams(vmem_limit_bytes=VMEM_LIMIT),
        cost_estimate=SHORT,
        name="add_history",
    )(scaled, mode_gain, scaled[None], mode_gain[None], *operands, image)


def copy_rows(source, out, held, sems):
    pieces = [pl.ds(k * ROWS, ROWS) for k in range(out.shape[0] // ROWS)]
    inward = [
        pltpu.make_async_copy(source.at[rows], held.at[rows], sems.at[0, k]) for k, rows in enumerate(pieces)
    ]
    outward = [
        pltpu.make_async_copy(held.at[rows], out.at[rows], sems.at[1, k]) for k, rows in enumerate(pieces)
    ]
    for copy in inward:
        copy.start()
    for copy, onward in zip(inward, outward):
        copy.wait()
        onward.start()
    for copy in outward:
        copy.wait()


def staged(kernel, name, shape, device, *arrays):
    return pl.pallas_call(
        kernel,
        in_specs=[pl.BlockSpec(memory_space=pltpu.SMEM)] * len(device)
        + [pl.BlockSpec(memory_space=pl.ANY)] * len(arrays),
        out_specs=pl.BlockSpec(memory_space=pl.ANY),
        out_shape=jax.ShapeDtypeStruct(shape, jnp.float32),
        scratch_shapes=[
            pltpu.VMEM(shape, jnp.float32),
            pltpu.SemaphoreType.DMA((2, math.prod(shape[:-1]) // ROWS)),
        ],
        compiler_params=pltpu.CompilerParams(vmem_limit_bytes=VMEM_LIMIT),
        cost_estimate=SHORT,
        name=name,
    )(*device, *arrays)


def place_of(me, slabs, depth):
    odd = me % 2
    half = me // 2
    back = slabs // 2 - 1 - half
    return [
        jnp.where(odd == 0, 0, depth - 1),
        jnp.where(odd == 0, depth - 1, 0),
        jnp.where(odd == 0, depth - 2, 1),
        jnp.where(odd == 0, half, back),
        jnp.where(odd == 1, half, back),
    ]


def rows_kernel(which, lo, device, field, out, held, sems):
    copy_rows(field.at[device[which], pl.ds(lo, out.shape[0])], out, held, sems)


def middle_kernel(lo, field, *refs):
    out, held, sems = refs[-3:]
    copy_rows(field.at[1, pl.ds(lo, out.shape[0])], out, held, sems)


def middle_rows(field, lo, hi, *token):
    kernel = functools.partial(middle_kernel, lo)
    return staged(kernel, "middle_rows", (hi - lo, field.shape[-1]), [], field, *token)


def rows_of(device, which, field, lo, hi):
    kernel = functools.partial(rows_kernel, which, lo)
    return staged(kernel, "rows_of", (hi - lo, field.shape[-1]), [device], field)


def pick_kernel(last, relayed_lo, own_lo, device, field, relayed, out, held, sems):
    count = out.shape[0]

    @pl.when(device[RANK] < last)
    def _():
        copy_rows(relayed.at[pl.ds(relayed_lo, count)], out, held, sems)

    @pl.when(device[RANK] >= last)
    def _():
        copy_rows(field.at[device[OUTER], pl.ds(own_lo, count)], out, held, sems)


def picked_rows(device, field, relayed, last, relayed_lo, own_lo, count):
    kernel = functools.partial(pick_kernel, last, relayed_lo, own_lo)
    return staged(kernel, "picked_rows", (count, field.shape[-1]), [device], field, relayed)


def head_kernel(field, out, held, sems):
    per_plane = BAND // ROWS
    for p in range(out.shape[0]):
        copy_rows(field.at[p, pl.ds(0, BAND)], out.at[p], held.at[p], sems.at[:, pl.ds(p * per_plane, per_plane)])


def head_of(field):
    depth, _, plane = field.shape
    return staged(head_kernel, "head_of", (depth, BAND, plane), [], field)


def join_kernel(*refs):
    arrays, (out, held, sems) = refs[:-3], refs[-3:]
    at = 0
    for array in arrays:
        rows = pl.ds(at, array.shape[0])
        copy_rows(array, out.at[rows], held.at[rows], sems.at[:, pl.ds(at // ROWS, array.shape[0] // ROWS)])
        at += array.shape[0]


def joined(arrays):
    shape = (sum(array.shape[0] for array in arrays), arrays[0].shape[1])
    return staged(join_kernel, "joined", shape, [], *arrays)


def plane_kernel(depth, shifts, absorption, field, *refs):
    image, masks = refs[-2:]
    plane = field.shape[-1]

    @pl.when(pl.program_id(0) == 0)
    def _():
        column = lax.broadcasted_iota(jnp.int32, (1, plane), 1)
        row_pos = column % NY
        for at, offset in enumerate(OFFSETS):
            weight = -DIFFUSION * STENCIL[offset + 2]
            moved = row_pos + offset
            masks[at : at + 1, :] = jnp.where((moved >= 0) & (moved < NY), weight, 0.0)
            at += len(OFFSETS)
            moved = column + offset * NY
            masks[at : at + 1, :] = jnp.where((moved >= 0) & (moved < plane), weight, 0.0)

    for p in range(depth):
        cells = field[p]
        total = (absorption[p][None, :] - 3.0 * DIFFUSION * STENCIL[2]) * cells
        for row, shift in enumerate(shifts):
            total = total + masks[row][None, :] * pltpu.roll(cells, (-shift) % plane, 1)
        for offset in OFFSETS:
            if 0 <= p + offset < depth:
                total = total + (-DIFFUSION * STENCIL[offset + 2]) * field[p + offset]
        image[p] = total


def plane_terms(absorption, field, image, start, end):
    depth, _, plane = field.shape
    shifts = tuple(OFFSETS) + tuple(offset * NY for offset in OFFSETS)
    first = start // ROWS
    slab = pl.BlockSpec((depth, ROWS, plane), lambda t: (0, first + t, 0))
    in_any = pl.BlockSpec(memory_space=pl.ANY)
    started = [] if image is None else [image]
    return pl.pallas_call(
        functools.partial(plane_kernel, depth, shifts),
        grid=((end - start) // ROWS,),
        in_specs=[pl.BlockSpec(absorption.shape, lambda t: (0, 0)), slab] + [in_any] * len(started),
        out_specs=slab,
        scratch_shapes=[pltpu.VMEM((len(shifts), plane), jnp.float32)],
        out_shape=jax.ShapeDtypeStruct(field.shape, jnp.float32),
        input_output_aliases={2: 0} if started else {},
        compiler_params=pltpu.CompilerParams(vmem_limit_bytes=VMEM_LIMIT),
        cost_estimate=SHORT,
        name="plane_terms",
    )(absorption, field, *started)


def update_kernel(change, planes_of, count, start, *refs):
    pieces = count // ROWS
    beside, (before, image, held, came, in_sems, came_sems, out_sems) = refs[:-7], refs[-7:]
    device = place_of(lax.axis_index("space"), lax.axis_size("space"), image.shape[0])
    planes = planes_of(device)

    def held_copy(p, k, out):
        there = pl.ds(start + k * ROWS, ROWS)
        here = held.at[p, pl.ds(k * ROWS, ROWS)]
        if out:
            return pltpu.make_async_copy(here, image.at[planes[p], there], out_sems.at[p, k])
        return pltpu.make_async_copy(before.at[planes[p], there], here, in_sems.at[p, k])

    def came_copy(i, k):
        source = beside[i].at[pl.ds(firsts[i] + k * ROWS, ROWS)]
        return pltpu.make_async_copy(source, came.at[i, pl.ds(k * ROWS, ROWS)], came_sems.at[i, k])

    firsts = change.firsts
    for k in range(pieces):
        for i in range(len(beside)):
            came_copy(i, k).start()
        for p in range(len(planes)):
            held_copy(p, k, False).start()
    for k in range(pieces):
        for i in range(len(beside)):
            came_copy(i, k).wait()
        for p in range(len(planes)):
            held_copy(p, k, False).wait()
        at = slice(k * ROWS, (k + 1) * ROWS)
        for p, added in enumerate(change(device, [came[i, at] for i in range(len(beside))])):
            held[p, at] += added
            held_copy(p, k, True).start()
    for k in range(pieces):
        for p in range(len(planes)):
            held_copy(p, k, True).wait()


class Change:
    def __init__(self, change, firsts):
        self.change, self.firsts = change, firsts

    def __call__(self, device, beside):
        return self.change(device, beside)


def update(name, change, planes_of, plane_count, arrays, image, start, count):
    plane = image.shape[-1]
    pieces = count // ROWS
    in_any = pl.BlockSpec(memory_space=pl.ANY)
    return pl.pallas_call(
        functools.partial(update_kernel, Change(change, [row for _, row in arrays]), planes_of, count, start),
        in_specs=[in_any] * (len(arrays) + 1),
        out_specs=in_any,
        out_shape=jax.ShapeDtypeStruct(image.shape, jnp.float32),
        scratch_shapes=[
            pltpu.VMEM((plane_count, count, plane), jnp.float32),
            pltpu.VMEM((len(arrays), count, plane), jnp.float32),
            pltpu.SemaphoreType.DMA((plane_count, pieces)),
            pltpu.SemaphoreType.DMA((len(arrays), pieces)),
            pltpu.SemaphoreType.DMA((plane_count, pieces)),
        ],
        input_output_aliases={len(arrays): 0},
        compiler_params=pltpu.CompilerParams(vmem_limit_bytes=VMEM_LIMIT),
        cost_estimate=SHORT,
        name=name,
    )(*[array for array, _ in arrays], image)


def add_halo(near, out_side, over_y, over_z, image, last, start, end):

    def change(device, beside):
        near, out_side, over_y, over_z = beside
        beyond = jnp.where(device[PARTNER_RANK] < last, over_y, over_z)
        return NEAR * beyond + FAR * out_side, FAR * beyond, FAR * near

    def planes_of(device):
        return device[OUTER], device[MIDDLE], device[INNER]

    arrays = (near, out_side, over_y, over_z)
    return update("add_halo", change, planes_of, 3, arrays, image, start, end - start)


def add_inner(beside, image, start):

    def change(device, beside):
        return NEAR * beside[0], FAR * beside[0]

    def planes_of(device):
        return device[INNER], device[MIDDLE]

    return update("add_inner", change, planes_of, 2, [(beside, 0)], image, start, beside.shape[0])


def ahead_kernel(start, image, out, sems):
    depth = image.shape[0]
    place = place_of(lax.axis_index("space"), lax.axis_size("space"), depth)
    copies = [
        pltpu.make_async_copy(image.at[plane, pl.ds(start, out.shape[1])], out.at[p], sems.at[p])
        for p, plane in enumerate((place[INNER], place[MIDDLE]))
    ]
    for copy in copies:
        copy.start()
    for copy in copies:
        copy.wait()


def rows_ahead(image, start):
    _, steps, plane = image.shape
    shape = (2, steps - start, plane)
    return pl.pallas_call(
        functools.partial(ahead_kernel, start),
        in_specs=[pl.BlockSpec(memory_space=pl.ANY)],
        out_specs=pl.BlockSpec(memory_space=pltpu.VMEM),
        out_shape=pltpu.VMEM(shape, jnp.float32),
        scratch_shapes=[pltpu.SemaphoreType.DMA((2,))],
        compiler_params=pltpu.CompilerParams(vmem_limit_bytes=VMEM_LIMIT),
        cost_estimate=SHORT,
        name="rows_ahead",
    )(image)


def last_kernel(start, parts, beside, ahead, image, token, out, held, sems):
    depth, _, plane = out.shape
    place = place_of(lax.axis_index("space"), lax.axis_size("space"), depth)
    width = plane // parts
    copies = []
    for c in range(parts):
        at = pl.ds(c * width, width)
        for p, (row, weight) in enumerate(((place[INNER], NEAR), (place[MIDDLE], FAR))):
            held[p, :, at] = ahead[p, :, at] + weight * beside[:, at]
            copy = pltpu.make_async_copy(
                held.at[p, :, at], out.at[row, pl.ds(start, held.shape[1]), at], sems.at[p, c]
            )
            copy.start()
            copies.append(copy)
    for copy in copies:
        copy.wait()


def add_last(beside, ahead, image, start, token):
    plane = image.shape[-1]
    parts = 4 if plane % 512 == 0 else 1
    in_vmem = pl.BlockSpec(memory_space=pltpu.VMEM)
    in_any = pl.BlockSpec(memory_space=pl.ANY)
    return pl.pallas_call(
        functools.partial(last_kernel, start, parts),
        in_specs=[in_vmem, in_vmem, in_any, in_any],
        out_specs=in_any,
        out_shape=jax.ShapeDtypeStruct(image.shape, jnp.float32),
        scratch_shapes=[pltpu.VMEM(ahead.shape, jnp.float32), pltpu.SemaphoreType.DMA((2, parts))],
        input_output_aliases={2: 0},
        compiler_params=pltpu.CompilerParams(vmem_limit_bytes=VMEM_LIMIT),
        cost_estimate=SHORT,
        name="add_last",
    )(beside, ahead, image, token)


def cuts(steps, pieces):
    marks = [ROWS * round(steps * i / pieces / ROWS) for i in range(pieces + 1)]
    return list(zip(marks[:-1], marks[1:]))


class Order:
    def __init__(self, token):
        self.token = token

    def __call__(self, value):
        value, self.token = lax.optimization_barrier((value, self.token))
        return value


def per_device(adjoint_field, absorption, mode_rates, mode_weights):
    steps, depth, plane = adjoint_field.shape
    groups = lax.axis_size("tm")
    slabs = lax.axis_size("space")
    pairs = slabs // 2
    me = lax.axis_index("space")
    field = adjoint_field.transpose(1, 0, 2)
    order = Order(mode_rates)

    swap = [(i, i ^ 1) for i in range(slabs)]
    outward = [(i, i - 2 if i % 2 == 0 else i + 2) for i in range(slabs)]
    outward = [(a, b) for a, b in outward if 0 <= b < slabs]
    onward = [(i, i + 2 if i % 2 == 0 else i - 2) for i in range(slabs)]
    onward = [(a, b) for a, b in onward if 0 <= b < slabs]

    def back(distance):
        return [(i, i - distance) for i in range(distance, groups)]


    def rank(i):
        return i // 2 if i % 2 == 0 else pairs - 1 - i // 2

    device = jnp.stack(place_of(me, slabs, depth)).astype(jnp.int32)

    def send(value, axis, route):
        return lax.ppermute(order(value), axis, route)

    def whole_rows(share):
        return ROWS * round(steps * share / ROWS)

    def between(*marks):
        return list(zip(marks[:-1], marks[1:]))

    mid_cuts = between(0, whole_rows(1 / 2), steps)
    out_cuts = cuts(steps, pairs)
    in_cuts = between(0, whole_rows(9 / 16), steps - ROWS, steps)
    plane_cuts = cuts(steps, 4)
    slots = pairs - 1

    def middle_send(k):
        token = [order.token] if k else []
        return send(middle_rows(field, *mid_cuts[k], *token), "space", swap)

    def outer_send(j):
        last = slots - j
        lo, hi = out_cuts[j]
        own_lo, own_hi = out_cuts[j + 1]
        first = out_cuts[(slots + 1) // 2][0]
        got, at = (relayed[0], lo) if lo < first else (relayed[1], lo - first)
        return send(
            picked_rows(order(device), field, got, last, at, own_lo, own_hi - own_lo), "space", swap
        )

    def outer_onward(parts):
        route = [(a, b) for a, b in onward if parts[-1] >= slots - rank(a ^ 1)]
        return send(y_out[parts[0]] if len(parts) == 1 else together, "space", route)

    def inner_send(k):
        return send(rows_of(order(device), INNER, field, *in_cuts[k]), "space", swap)

    def relay(lo, hi):
        return send(rows_of(order(device), OUTER, field, lo, hi), "space", outward)

    y_steps = [functools.partial(middle_send, k) for k in range(len(mid_cuts))]
    y_steps += [functools.partial(outer_send, j) for j in range(slots)]
    y_steps += [functools.partial(inner_send, k) for k in range(len(in_cuts))]
    sent = []

    def next_y():
        if len(sent) < len(y_steps):
            sent.append(y_steps[len(sent)]())

    scaled, mode_gain = mode_tables(mode_rates, mode_weights, steps * groups)
    next_y()
    next_y()
    first = out_cuts[(slots + 1) // 2][0]
    relayed = [relay(0, first)]
    head = send(head_of(order(field)), "tm", back(1))
    sums = mode_sums(order(scaled), field)
    aways = [1]
    later = [send(sums, "tm", back(1))]

    def plane(k, image):
        return order(plane_terms(order(absorption), field, image, *plane_cuts[k]))

    image = plane(0, None)
    y_mid = [order(sent[0])]
    z_mid = [send(y_mid[0], "space", onward)]
    relayed[0] = order(relayed[0])
    next_y()
    head = order(head)
    later[0] = order(later[0])
    if first < out_cuts[slots][0]:
        relayed.append(relay(first, out_cuts[slots][0]))
    while 2 * aways[-1] < groups:
        if len(aways) > 1:
            later[-1] = order(later[-1])
        sums = carried(order(scaled), aways[-1] * steps, sums, later[-1])
        aways.append(2 * aways[-1])
        later.append(send(sums, "tm", back(aways[-1])))

    image = plane(1, image)
    y_mid.append(order(sent[1]))
    next_y()
    image = plane(2, image)

    def halo(q, image):
        lo, hi = out_cuts[q]
        over_z = y_out[0] if q == 0 else z_last if q == slots else z_most
        at_z = out_cuts[q - 1][0] if 0 < q < slots else 0
        over_y = (y_out[q], 0) if q < slots else (over_z, 0)
        if q == 0:
            over_z = jnp.zeros_like(over_z)
        for k, (start, end) in enumerate(mid_cuts):
            a, b = max(lo, start), min(hi, end)
            if a < b:
                image = add_halo(
                    (y_mid[k], a - start), (z_mid[k], a - start), (over_y[0], a - lo),
                    (over_z, at_z + a - lo), image, slots - q, a, b,
                )
        return order(image)

    y_out = []
    def inner(k, image):
        return order(add_inner(y_in[k], image, in_cuts[k][0]))

    for j in range(slots):
        y_out.append(order(sent[2 + j]))
        if j == 0:
            relayed[1:] = order(relayed[1:])
        if j < slots - 1:
            next_y()
        if j == 0:
            z_mid.append(send(y_mid[1], "space", onward))
            image = plane(3, image)
        if j == min(1, slots - 1):
            later[1:] = order(later[1:])
        if j == slots - 2:
            together = joined(order(list(y_out)))
    z_mid[0] = order(z_mid[0])
    most = list(range(slots - 1))
    z_most = outer_onward(most) if most else None
    next_y()
    z_mid[1] = order(z_mid[1])
    z_last = outer_onward([slots - 1])
    image = halo(0, image)
    image = order(add_history(order(scaled), mode_gain, field, head, aways, later, image))
    y_in = [order(sent[2 + slots])]
    next_y()
    image = inner(0, image)
    if most:
        z_most = order(z_most)
    for q in range(1, slots):
        image = halo(q, image)
    z_last = order(z_last)
    image = halo(slots, image)
    last = in_cuts[-1][0]
    ahead = order(rows_ahead(image, last))
    for k in range(1, len(in_cuts) - 1):
        y_in.append(order(sent[2 + slots + k]))
        image = inner(k, image)
    image = add_last(order(sent[-1]), ahead, image, last, order.token)
    return image.transpose(1, 0, 2)


def solution(mesh):
    return jax.shard_map(
        per_device,
        mesh=mesh,
        in_specs=(P("tm", "space", None), P("space", None), P(), P()),
        out_specs=P("tm", "space", None),
        check_vma=False,
    )
```

```python
import functools
import math

import jax
import jax.numpy as jnp
from jax import lax
from jax.experimental import pallas as pl
from jax.experimental.pallas import tpu as pltpu
from jax.sharding import PartitionSpec as P
import numpy as np

NY = 96
BAND = 16

DIFFUSION = 0.2
ORDER_EXP = 0.4
STENCIL = (-1.0 / 12.0, 16.0 / 12.0, -30.0 / 12.0, 16.0 / 12.0, -1.0 / 12.0)
NEAR = -DIFFUSION * STENCIL[1]
FAR = -DIFFUSION * STENCIL[0]
OFFSETS = (-2, -1, 1, 2)
ROWS = 8
VMEM_LIMIT = 48 * 1024 * 1024
SHORT = pl.CostEstimate(flops=1, bytes_accessed=1, transcendentals=0)

OUTER, INNER, MIDDLE, RANK, PARTNER_RANK = range(5)


def mode_tables(mode_rates, mode_weights, total_steps):
    scaled = mode_rates / total_steps
    mode_gain = mode_weights * jnp.sqrt(-jnp.expm1(-2.0 * scaled))
    return scaled, mode_gain


def caputo_weights():
    grown = np.arange(BAND + 1, dtype=np.float64) ** ORDER_EXP
    increments = grown[1:] - grown[:-1]
    return [float(w) for w in np.diff(increments, prepend=0.0)]


def dot(a, b):
    return jnp.dot(a, b, precision=lax.Precision.HIGHEST, preferred_element_type=jnp.float32)


def tile_of(plane):
    for count in range(4, plane + 1):
        if plane % count == 0 and (plane // count) % 128 == 0:
            return plane // count
    return plane


def sums_kernel(scaled, field, sums, projector):
    modes, steps = projector.shape

    @pl.when((pl.program_id(0) == 0) & (pl.program_id(1) == 0))
    def _():
        pos = lax.broadcasted_iota(jnp.int32, (1, steps), 1).astype(jnp.float32)
        for j in range(modes):
            projector[j : j + 1, :] = jnp.exp(-scaled[j] * pos)

    sums[...] = dot(projector[...], field[...])


def mode_sums(scaled, field):
    depth, steps, plane = field.shape
    modes = scaled.shape[0]
    tile = tile_of(plane)
    return pl.pallas_call(
        sums_kernel,
        grid=(depth, plane // tile),
        in_specs=[
            pl.BlockSpec(memory_space=pltpu.SMEM),
            pl.BlockSpec((None, steps, tile), lambda p, c: (p, 0, c)),
        ],
        out_specs=pl.BlockSpec((None, modes, tile), lambda p, c: (p, 0, c)),
        out_shape=jax.ShapeDtypeStruct((depth, modes, plane), jnp.float32),
        scratch_shapes=[pltpu.VMEM((modes, steps), jnp.float32)],
        compiler_params=pltpu.CompilerParams(vmem_limit_bytes=VMEM_LIMIT),
        cost_estimate=SHORT,
        name="mode_sums",
    )(scaled, field)


def carry_kernel(steps, scaled, sums, later, total):
    for j in range(total.shape[0]):
        decay = jnp.exp(jnp.full((1, total.shape[1]), -scaled[j] * steps, jnp.float32))
        total[j : j + 1, :] = sums[j : j + 1, :] + decay * later[j : j + 1, :]


def carried(scaled, steps, sums, later):
    depth, _, plane = sums.shape
    modes = scaled.shape[0]
    part = pl.BlockSpec((None, modes, plane), lambda p: (p, 0, 0))
    return pl.pallas_call(
        functools.partial(carry_kernel, steps),
        grid=(depth,),
        in_specs=[pl.BlockSpec(memory_space=pltpu.SMEM), part, part],
        out_specs=part,
        out_shape=jax.ShapeDtypeStruct((depth, modes, plane), jnp.float32),
        cost_estimate=SHORT,
        name="carried",
    )(scaled, sums, later)


def fill_tables(steps, aways, scaled, mode_gain, scaled_row, gain_row, table):
    near_weights = caputo_weights()
    modes = scaled.shape[0]

    def lags(columns, ahead):
        row = lax.broadcasted_iota(jnp.int32, (steps, columns), 0)
        return lax.broadcasted_iota(jnp.int32, (steps, columns), 1) - row + ahead

    def far_of(lag):
        distance = jnp.maximum(lag, 0).astype(jnp.float32)
        far = jnp.zeros(lag.shape, jnp.float32)
        for j in range(modes):
            far = far + mode_gain[j] * jnp.exp(-scaled[j] * distance)
        return far

    def near_of(lag):
        near = jnp.zeros(lag.shape, jnp.float32)
        for k, weight in enumerate(near_weights):
            near = jnp.where(lag == k, weight, near)
        return near

    lag = lags(steps, 0)
    table[:, :steps] = jnp.where(lag >= BAND, far_of(lag), near_of(lag))
    lag = lags(BAND, steps)
    table[:, steps : steps + BAND] = jnp.where(lag < BAND, near_of(lag) - far_of(lag), 0.0)
    row = lax.broadcasted_iota(jnp.int32, (steps, modes), 0)
    for k, away in enumerate(aways):
        at = steps + BAND + k * modes
        distance = (away * steps - row).astype(jnp.float32)
        table[:, at : at + modes] = gain_row[...] * jnp.exp(-scaled_row[...] * distance)


def history_kernel(aways, scaled, mode_gain, scaled_row, gain_row, field, *refs):
    parts, (before, image, table, stacked) = refs[: 1 + len(aways)], refs[1 + len(aways) :]
    steps = field.shape[0]

    @pl.when((pl.program_id(0) == 0) & (pl.program_id(1) == 0))
    def _():
        fill_tables(steps, aways, scaled, mode_gain, scaled_row, gain_row, table)

    stacked[:steps, :] = field[...]
    at = steps
    for part in parts:
        stacked[at : at + part.shape[0], :] = part[...]
        at += part.shape[0]
    image[...] = before[...] + dot(table[...], stacked[...])


def add_history(scaled, mode_gain, field, head, aways, later, image):
    depth, steps, plane = field.shape
    modes = scaled.shape[0]
    tile = tile_of(plane)
    operands = (field, head, *later)
    rows = sum(array.shape[1] for array in operands)
    smem = pl.BlockSpec(memory_space=pltpu.SMEM)
    whole = pl.BlockSpec((1, modes), lambda p, c: (0, 0))
    part = lambda p, c: (p, 0, c)
    return pl.pallas_call(
        functools.partial(history_kernel, aways),
        grid=(depth, plane // tile),
        in_specs=[
            smem,
            smem,
            whole,
            whole,
            *[pl.BlockSpec((None, array.shape[1], tile), part) for array in (*operands, image)],
        ],
        out_specs=pl.BlockSpec((None, steps, tile), part),
        out_shape=jax.ShapeDtypeStruct(field.shape, jnp.float32),
        input_output_aliases={4 + len(operands): 0},
        scratch_shapes=[pltpu.VMEM((steps, rows), jnp.float32), pltpu.VMEM((rows, tile), jnp.float32)],
        compiler_params=pltpu.CompilerParams(vmem_limit_bytes=VMEM_LIMIT),
        cost_estimate=SHORT,
        name="add_history",
    )(scaled, mode_gain, scaled[None], mode_gain[None], *operands, image)


def copy_rows(source, out, held, sems):
    pieces = [pl.ds(k * ROWS, ROWS) for k in range(out.shape[0] // ROWS)]
    inward = [
        pltpu.make_async_copy(source.at[rows], held.at[rows], sems.at[0, k]) for k, rows in enumerate(pieces)
    ]
    outward = [
        pltpu.make_async_copy(held.at[rows], out.at[rows], sems.at[1, k]) for k, rows in enumerate(pieces)
    ]
    for copy in inward:
        copy.start()
    for copy, onward in zip(inward, outward):
        copy.wait()
        onward.start()
    for copy in outward:
        copy.wait()


def staged(kernel, name, shape, device, *arrays):
    return pl.pallas_call(
        kernel,
        in_specs=[pl.BlockSpec(memory_space=pltpu.SMEM)] * len(device)
        + [pl.BlockSpec(memory_space=pl.ANY)] * len(arrays),
        out_specs=pl.BlockSpec(memory_space=pl.ANY),
        out_shape=jax.ShapeDtypeStruct(shape, jnp.float32),
        scratch_shapes=[
            pltpu.VMEM(shape, jnp.float32),
            pltpu.SemaphoreType.DMA((2, math.prod(shape[:-1]) // ROWS)),
        ],
        compiler_params=pltpu.CompilerParams(vmem_limit_bytes=VMEM_LIMIT),
        cost_estimate=SHORT,
        name=name,
    )(*device, *arrays)


def place_of(me, slabs, depth):
    odd = me % 2
    half = me // 2
    back = slabs // 2 - 1 - half
    return [
        jnp.where(odd == 0, 0, depth - 1),
        jnp.where(odd == 0, depth - 1, 0),
        jnp.where(odd == 0, depth - 2, 1),
        jnp.where(odd == 0, half, back),
        jnp.where(odd == 1, half, back),
    ]


def rows_kernel(which, lo, device, field, out, held, sems):
    copy_rows(field.at[device[which], pl.ds(lo, out.shape[0])], out, held, sems)


def middle_kernel(lo, field, *refs):
    out, held, sems = refs[-3:]
    copy_rows(field.at[1, pl.ds(lo, out.shape[0])], out, held, sems)


def middle_rows(field, lo, hi, *token):
    kernel = functools.partial(middle_kernel, lo)
    return staged(kernel, "middle_rows", (hi - lo, field.shape[-1]), [], field, *token)


def rows_of(device, which, field, lo, hi):
    kernel = functools.partial(rows_kernel, which, lo)
    return staged(kernel, "rows_of", (hi - lo, field.shape[-1]), [device], field)


def pick_kernel(last, relayed_lo, own_lo, device, field, relayed, out, held, sems):
    count = out.shape[0]

    @pl.when(device[RANK] < last)
    def _():
        copy_rows(relayed.at[pl.ds(relayed_lo, count)], out, held, sems)

    @pl.when(device[RANK] >= last)
    def _():
        copy_rows(field.at[device[OUTER], pl.ds(own_lo, count)], out, held, sems)


def picked_rows(device, field, relayed, last, relayed_lo, own_lo, count):
    kernel = functools.partial(pick_kernel, last, relayed_lo, own_lo)
    return staged(kernel, "picked_rows", (count, field.shape[-1]), [device], field, relayed)


def head_kernel(field, out, held, sems):
    per_plane = BAND // ROWS
    for p in range(out.shape[0]):
        copy_rows(field.at[p, pl.ds(0, BAND)], out.at[p], held.at[p], sems.at[:, pl.ds(p * per_plane, per_plane)])


def head_of(field):
    depth, _, plane = field.shape
    return staged(head_kernel, "head_of", (depth, BAND, plane), [], field)


def join_kernel(*refs):
    arrays, (out, held, sems) = refs[:-3], refs[-3:]
    at = 0
    for array in arrays:
        rows = pl.ds(at, array.shape[0])
        copy_rows(array, out.at[rows], held.at[rows], sems.at[:, pl.ds(at // ROWS, array.shape[0] // ROWS)])
        at += array.shape[0]


def joined(arrays):
    shape = (sum(array.shape[0] for array in arrays), arrays[0].shape[1])
    return staged(join_kernel, "joined", shape, [], *arrays)


def plane_kernel(depth, shifts, absorption, field, *refs):
    image, masks = refs[-2:]
    plane = field.shape[-1]

    @pl.when(pl.program_id(0) == 0)
    def _():
        column = lax.broadcasted_iota(jnp.int32, (1, plane), 1)
        row_pos = column % NY
        for at, offset in enumerate(OFFSETS):
            weight = -DIFFUSION * STENCIL[offset + 2]
            moved = row_pos + offset
            masks[at : at + 1, :] = jnp.where((moved >= 0) & (moved < NY), weight, 0.0)
            at += len(OFFSETS)
            moved = column + offset * NY
            masks[at : at + 1, :] = jnp.where((moved >= 0) & (moved < plane), weight, 0.0)

    for p in range(depth):
        cells = field[p]
        total = (absorption[p][None, :] - 3.0 * DIFFUSION * STENCIL[2]) * cells
        for row, shift in enumerate(shifts):
            total = total + masks[row][None, :] * pltpu.roll(cells, (-shift) % plane, 1)
        for offset in OFFSETS:
            if 0 <= p + offset < depth:
                total = total + (-DIFFUSION * STENCIL[offset + 2]) * field[p + offset]
        image[p] = total


def plane_terms(absorption, field, image, start, end):
    depth, _, plane = field.shape
    shifts = tuple(OFFSETS) + tuple(offset * NY for offset in OFFSETS)
    first = start // ROWS
    slab = pl.BlockSpec((depth, ROWS, plane), lambda t: (0, first + t, 0))
    in_any = pl.BlockSpec(memory_space=pl.ANY)
    started = [] if image is None else [image]
    return pl.pallas_call(
        functools.partial(plane_kernel, depth, shifts),
        grid=((end - start) // ROWS,),
        in_specs=[pl.BlockSpec(absorption.shape, lambda t: (0, 0)), slab] + [in_any] * len(started),
        out_specs=slab,
        scratch_shapes=[pltpu.VMEM((len(shifts), plane), jnp.float32)],
        out_shape=jax.ShapeDtypeStruct(field.shape, jnp.float32),
        input_output_aliases={2: 0} if started else {},
        compiler_params=pltpu.CompilerParams(vmem_limit_bytes=VMEM_LIMIT),
        cost_estimate=SHORT,
        name="plane_terms",
    )(absorption, field, *started)


def update_kernel(change, planes_of, count, start, *refs):
    pieces = count // ROWS
    beside, (before, image, held, came, in_sems, came_sems, out_sems) = refs[:-7], refs[-7:]
    device = place_of(lax.axis_index("space"), lax.axis_size("space"), image.shape[0])
    planes = planes_of(device)

    def held_copy(p, k, out):
        there = pl.ds(start + k * ROWS, ROWS)
        here = held.at[p, pl.ds(k * ROWS, ROWS)]
        if out:
            return pltpu.make_async_copy(here, image.at[planes[p], there], out_sems.at[p, k])
        return pltpu.make_async_copy(before.at[planes[p], there], here, in_sems.at[p, k])

    def came_copy(i, k):
        source = beside[i].at[pl.ds(firsts[i] + k * ROWS, ROWS)]
        return pltpu.make_async_copy(source, came.at[i, pl.ds(k * ROWS, ROWS)], came_sems.at[i, k])

    firsts = change.firsts
    for k in range(pieces):
        for i in range(len(beside)):
            came_copy(i, k).start()
        for p in range(len(planes)):
            held_copy(p, k, False).start()
    for k in range(pieces):
        for i in range(len(beside)):
            came_copy(i, k).wait()
        for p in range(len(planes)):
            held_copy(p, k, False).wait()
        at = slice(k * ROWS, (k + 1) * ROWS)
        for p, added in enumerate(change(device, [came[i, at] for i in range(len(beside))])):
            held[p, at] += added
            held_copy(p, k, True).start()
    for k in range(pieces):
        for p in range(len(planes)):
            held_copy(p, k, True).wait()


class Change:
    def __init__(self, change, firsts):
        self.change, self.firsts = change, firsts

    def __call__(self, device, beside):
        return self.change(device, beside)


def update(name, change, planes_of, plane_count, arrays, image, start, count):
    plane = image.shape[-1]
    pieces = count // ROWS
    in_any = pl.BlockSpec(memory_space=pl.ANY)
    return pl.pallas_call(
        functools.partial(update_kernel, Change(change, [row for _, row in arrays]), planes_of, count, start),
        in_specs=[in_any] * (len(arrays) + 1),
        out_specs=in_any,
        out_shape=jax.ShapeDtypeStruct(image.shape, jnp.float32),
        scratch_shapes=[
            pltpu.VMEM((plane_count, count, plane), jnp.float32),
            pltpu.VMEM((len(arrays), count, plane), jnp.float32),
            pltpu.SemaphoreType.DMA((plane_count, pieces)),
            pltpu.SemaphoreType.DMA((len(arrays), pieces)),
            pltpu.SemaphoreType.DMA((plane_count, pieces)),
        ],
        input_output_aliases={len(arrays): 0},
        compiler_params=pltpu.CompilerParams(vmem_limit_bytes=VMEM_LIMIT),
        cost_estimate=SHORT,
        name=name,
    )(*[array for array, _ in arrays], image)


def add_halo(near, out_side, over_y, over_z, image, last, start, end):

    def change(device, beside):
        near, out_side, over_y, over_z = beside
        beyond = jnp.where(device[PARTNER_RANK] < last, over_y, over_z)
        return NEAR * beyond + FAR * out_side, FAR * beyond, FAR * near

    def planes_of(device):
        return device[OUTER], device[MIDDLE], device[INNER]

    arrays = (near, out_side, over_y, over_z)
    return update("add_halo", change, planes_of, 3, arrays, image, start, end - start)


def add_inner(beside, image, start):

    def change(device, beside):
        return NEAR * beside[0], FAR * beside[0]

    def planes_of(device):
        return device[INNER], device[MIDDLE]

    return update("add_inner", change, planes_of, 2, [(beside, 0)], image, start, beside.shape[0])


def ahead_kernel(start, image, out, sems):
    depth = image.shape[0]
    place = place_of(lax.axis_index("space"), lax.axis_size("space"), depth)
    copies = [
        pltpu.make_async_copy(image.at[plane, pl.ds(start, out.shape[1])], out.at[p], sems.at[p])
        for p, plane in enumerate((place[INNER], place[MIDDLE]))
    ]
    for copy in copies:
        copy.start()
    for copy in copies:
        copy.wait()


def rows_ahead(image, start):
    _, steps, plane = image.shape
    shape = (2, steps - start, plane)
    return pl.pallas_call(
        functools.partial(ahead_kernel, start),
        in_specs=[pl.BlockSpec(memory_space=pl.ANY)],
        out_specs=pl.BlockSpec(memory_space=pltpu.VMEM),
        out_shape=pltpu.VMEM(shape, jnp.float32),
        scratch_shapes=[pltpu.SemaphoreType.DMA((2,))],
        compiler_params=pltpu.CompilerParams(vmem_limit_bytes=VMEM_LIMIT),
        cost_estimate=SHORT,
        name="rows_ahead",
    )(image)


def last_kernel(start, parts, beside, ahead, image, token, out, held, sems):
    depth, _, plane = out.shape
    place = place_of(lax.axis_index("space"), lax.axis_size("space"), depth)
    width = plane // parts
    copies = []
    for c in range(parts):
        at = pl.ds(c * width, width)
        for p, (row, weight) in enumerate(((place[INNER], NEAR), (place[MIDDLE], FAR))):
            held[p, :, at] = ahead[p, :, at] + weight * beside[:, at]
            copy = pltpu.make_async_copy(
                held.at[p, :, at], out.at[row, pl.ds(start, held.shape[1]), at], sems.at[p, c]
            )
            copy.start()
            copies.append(copy)
    for copy in copies:
        copy.wait()


def add_last(beside, ahead, image, start, token):
    plane = image.shape[-1]
    parts = 4 if plane % 512 == 0 else 1
    in_vmem = pl.BlockSpec(memory_space=pltpu.VMEM)
    in_any = pl.BlockSpec(memory_space=pl.ANY)
    return pl.pallas_call(
        functools.partial(last_kernel, start, parts),
        in_specs=[in_vmem, in_vmem, in_any, in_any],
        out_specs=in_any,
        out_shape=jax.ShapeDtypeStruct(image.shape, jnp.float32),
        scratch_shapes=[pltpu.VMEM(ahead.shape, jnp.float32), pltpu.SemaphoreType.DMA((2, parts))],
        input_output_aliases={2: 0},
        compiler_params=pltpu.CompilerParams(vmem_limit_bytes=VMEM_LIMIT),
        cost_estimate=SHORT,
        name="add_last",
    )(beside, ahead, image, token)


def cuts(steps, pieces):
    marks = [ROWS * round(steps * i / pieces / ROWS) for i in range(pieces + 1)]
    return list(zip(marks[:-1], marks[1:]))


class Order:
    def __init__(self, token):
        self.token = token

    def __call__(self, value):
        value, self.token = lax.optimization_barrier((value, self.token))
        return value


def per_device(adjoint_field, absorption, mode_rates, mode_weights):
    steps, depth, plane = adjoint_field.shape
    groups = lax.axis_size("tm")
    slabs = lax.axis_size("space")
    pairs = slabs // 2
    me = lax.axis_index("space")
    field = adjoint_field.transpose(1, 0, 2)
    order = Order(mode_rates)

    swap = [(i, i ^ 1) for i in range(slabs)]
    outward = [(i, i - 2 if i % 2 == 0 else i + 2) for i in range(slabs)]
    outward = [(a, b) for a, b in outward if 0 <= b < slabs]
    onward = [(i, i + 2 if i % 2 == 0 else i - 2) for i in range(slabs)]
    onward = [(a, b) for a, b in onward if 0 <= b < slabs]

    def back(distance):
        return [(i, i - distance) for i in range(distance, groups)]


    def rank(i):
        return i // 2 if i % 2 == 0 else pairs - 1 - i // 2

    device = jnp.stack(place_of(me, slabs, depth)).astype(jnp.int32)

    def send(value, axis, route):
        return lax.ppermute(order(value), axis, route)

    def whole_rows(share):
        return ROWS * round(steps * share / ROWS)

    def between(*marks):
        return list(zip(marks[:-1], marks[1:]))

    mid_cuts = between(0, whole_rows(1 / 2), steps)
    out_cuts = cuts(steps, pairs)
    in_cuts = between(0, whole_rows(9 / 16), steps - 2 * ROWS, steps)
    plane_cuts = cuts(steps, 4)
    slots = pairs - 1

    def middle_send(k):
        token = [order.token] if k else []
        return send(middle_rows(field, *mid_cuts[k], *token), "space", swap)

    def outer_send(j):
        last = slots - j
        lo, hi = out_cuts[j]
        own_lo, own_hi = out_cuts[j + 1]
        first = out_cuts[(slots + 1) // 2][0]
        got, at = (relayed[0], lo) if lo < first else (relayed[1], lo - first)
        return send(
            picked_rows(order(device), field, got, last, at, own_lo, own_hi - own_lo), "space", swap
        )

    def outer_onward(parts):
        route = [(a, b) for a, b in onward if parts[-1] >= slots - rank(a ^ 1)]
        return send(y_out[parts[0]] if len(parts) == 1 else together, "space", route)

    def inner_send(k):
        return send(rows_of(order(device), INNER, field, *in_cuts[k]), "space", swap)

    def relay(lo, hi):
        return send(rows_of(order(device), OUTER, field, lo, hi), "space", outward)

    y_steps = [functools.partial(middle_send, k) for k in range(len(mid_cuts))]
    y_steps += [functools.partial(outer_send, j) for j in range(slots)]
    y_steps += [functools.partial(inner_send, k) for k in range(len(in_cuts))]
    sent = []

    def next_y():
        if len(sent) < len(y_steps):
            sent.append(y_steps[len(sent)]())

    scaled, mode_gain = mode_tables(mode_rates, mode_weights, steps * groups)
    next_y()
    next_y()
    first = out_cuts[(slots + 1) // 2][0]
    relayed = [relay(0, first)]
    head = send(head_of(order(field)), "tm", back(1))
    sums = mode_sums(order(scaled), field)
    aways = [1]
    later = [send(sums, "tm", back(1))]

    def plane(k, image):
        return order(plane_terms(order(absorption), field, image, *plane_cuts[k]))

    image = plane(0, None)
    y_mid = [order(sent[0])]
    z_mid = [send(y_mid[0], "space", onward)]
    relayed[0] = order(relayed[0])
    next_y()
    head = order(head)
    later[0] = order(later[0])
    if first < out_cuts[slots][0]:
        relayed.append(relay(first, out_cuts[slots][0]))
    while 2 * aways[-1] < groups:
        if len(aways) > 1:
            later[-1] = order(later[-1])
        sums = carried(order(scaled), aways[-1] * steps, sums, later[-1])
        aways.append(2 * aways[-1])
        later.append(send(sums, "tm", back(aways[-1])))

    image = plane(1, image)
    y_mid.append(order(sent[1]))
    next_y()
    image = plane(2, image)

    def halo(q, image):
        lo, hi = out_cuts[q]
        over_z = y_out[0] if q == 0 else z_last if q == slots else z_most
        at_z = out_cuts[q - 1][0] if 0 < q < slots else 0
        over_y = (y_out[q], 0) if q < slots else (over_z, 0)
        if q == 0:
            over_z = jnp.zeros_like(over_z)
        for k, (start, end) in enumerate(mid_cuts):
            a, b = max(lo, start), min(hi, end)
            if a < b:
                image = add_halo(
                    (y_mid[k], a - start), (z_mid[k], a - start), (over_y[0], a - lo),
                    (over_z, at_z + a - lo), image, slots - q, a, b,
                )
        return order(image)

    y_out = []
    def inner(k, image):
        return order(add_inner(y_in[k], image, in_cuts[k][0]))

    for j in range(slots):
        y_out.append(order(sent[2 + j]))
        if j == 0:
            relayed[1:] = order(relayed[1:])
        if j < slots - 1:
            next_y()
        if j == 0:
            z_mid.append(send(y_mid[1], "space", onward))
            image = plane(3, image)
        if j == min(1, slots - 1):
            later[1:] = order(later[1:])
        if j == slots - 2:
            together = joined(order(list(y_out)))
    z_mid[0] = order(z_mid[0])
    most = list(range(slots - 1))
    z_most = outer_onward(most) if most else None
    next_y()
    z_mid[1] = order(z_mid[1])
    z_last = outer_onward([slots - 1])
    image = halo(0, image)
    image = order(add_history(order(scaled), mode_gain, field, head, aways, later, image))
    y_in = [order(sent[2 + slots])]
    next_y()
    image = inner(0, image)
    if most:
        z_most = order(z_most)
    for q in range(1, slots):
        image = halo(q, image)
    z_last = order(z_last)
    image = halo(slots, image)
    last = in_cuts[-1][0]
    ahead = order(rows_ahead(image, last))
    for k in range(1, len(in_cuts) - 1):
        y_in.append(order(sent[2 + slots + k]))
        image = inner(k, image)
    image = add_last(order(sent[-1]), ahead, image, last, order.token)
    return image.transpose(1, 0, 2)


def solution(mesh):
    return jax.shard_map(
        per_device,
        mesh=mesh,
        in_specs=(P("tm", "space", None), P("space", None), P(), P()),
        out_specs=P("tm", "space", None),
        check_vma=False,
    )
```
